32 devices in a mesh: dp: 2 (over core), ctx: 4 (over z), head: 4 (over y, x).
Axes of the slice: x: 2, y: 2, z: 4, core: 2. Of those that a mesh axis runs over, the one named last changes fastest.
Arguments:
- queries: bfloat16 [2, 1024, 2048], P('dp', 'ctx', 'head'), may hold values from -6 to 6
- keys: bfloat16 [2, 1024, 2048], P('dp', 'ctx', 'head'), may hold values from -6 to 6
- values: bfloat16 [2, 1024, 2048], P('dp', 'ctx', 'head'), may hold values from -32 to 32
- spikes: int32 [2, 1024, 2048], P('dp', 'ctx', 'head'), may hold values 0 or 1
- gain: float32 [2048], P('head'), may hold values from 0.25 to 1.75
- upstream: bfloat16 [2, 1024, 2048], P('dp', 'ctx', 'head'), may hold values from -16 to 16
Outputs:
- grad_queries: bfloat16 [2, 1024, 2048], P('dp', 'ctx', 'head')
- grad_keys: bfloat16 [2, 1024, 2048], P('dp', 'ctx', 'head')
- grad_values: bfloat16 [2, 1024, 2048], P('dp', 'ctx', 'head')
- grad_gain: float32 [2048], P('head')
The draws below stay inside these ranges and needn't reach their ends.
All inputs are finite; a program needn't handle non-finite values. No bound on the sum of `spikes` on one device may be relied on, other than what follows from the above.
Results may differ from the reference program's by a relative error of at most 0.0058.
Values sent between devices are 32-bit elements; how exact they have to be, the bound alone decides.
No kernel may reach another device: no remote copies, remote signals or barrier semaphores. Data moves between devices by JAX's collectives and lax.ppermute only.
A program may use at most 64 MiB of HBM per device.

```python
import math
import jax
import jax.numpy as jnp
from jax import lax

DH = 128
HEADS = 16
TOK_DEV = 256
SEQS = 2
LEN = 1024


def draw_values(key, part):
    key = jax.random.fold_in(key, 11)
    key_chan, key_main = jax.random.split(key)
    width = HEADS * DH
    head_pos = (jnp.arange(width) // DH).astype(jnp.float32) / max(HEADS - 1, 1)
    chan_log = jax.random.uniform(key_chan, (width,), jnp.float32, -1.2, 1.098)
    ramp = 3.0 ** (0.5 * head_pos)
    main = jnp.clip(jax.random.normal(key_main, (SEQS, LEN, width), jnp.float32), -6.0, 6.0)
    return (main * jnp.exp(chan_log) * ramp).astype(jnp.bfloat16)


def draw_upstream(key, part):
    key = jax.random.fold_in(key, 23)
    key_row, key_main = jax.random.split(key, 2)
    width = HEADS * DH
    row_log = jax.random.uniform(key_row, (SEQS, LEN, 1), jnp.float32, -1.2, 1.098)
    main = jnp.clip(jax.random.normal(key_main, (SEQS, LEN, width), jnp.float32), -5.0, 5.0)
    return (main * jnp.exp(row_log)).astype(jnp.bfloat16)


def touch_ends(values, stream_key, smallest, largest):
    extent = values.shape
    index_at = [jax.random.randint(jax.random.fold_in(stream_key, axis), (), 0, extent[axis]) for axis in range(len(extent))]
    values = values.at[tuple(index_at)].set(smallest)
    longest = extent.index(max(extent))
    index_at[longest] = (index_at[longest] + 1) % extent[longest]
    return values.at[tuple(index_at)].set(largest)


def steps_of(own_key, shape, cuts, least, high):
    level = 1.0
    for position, blocks in cuts:
        steps = jax.random.uniform(jax.random.fold_in(jax.random.fold_in(own_key, 6), position), (blocks,), jnp.float32, least / len(cuts), high / len(cuts))
        level = level * jnp.repeat(jnp.exp(steps), shape[position] // blocks).reshape((-1,) + (1,) * (len(shape) - 1 - position))
    return level


def scatter_about(key, extent, scale, reach, cuts=(), held_as=jnp.bfloat16):
    loudness = steps_of(key, extent, cuts, -0.22, 0.18) if cuts else 1.0
    entries = jax.random.normal(key, extent, jnp.float32) * scale * loudness
    return jnp.minimum(jnp.maximum(entries, -reach), reach).astype(held_as)


def setup_inputs(seed: int = 0) -> dict:
    seeds = jax.random.split(jax.random.key(seed), 7)
    return {
        "queries": scatter_about(seeds[0], (SEQS, LEN, HEADS * DH), 1.0, 6.0, ((0, 2), (1, 4), (2, 4))),
        "keys": scatter_about(seeds[1], (SEQS, LEN, HEADS * DH), 1.0, 6.0, ((0, 2), (1, 4), (2, 4))),
        "values": draw_values(jax.random.fold_in(seeds[6], 71), 0),
        "spikes": touch_ends((jax.random.randint(seeds[3], (SEQS, LEN, HEADS * DH), 0, 2) < 1).astype(jnp.int32), jax.random.fold_in(seeds[3], 1), 0, 1),
        "gain": jnp.clip(1.0 + 0.15 * jax.random.normal(seeds[4], (HEADS * DH,), jnp.float32), 0.25, 1.75),
        "upstream": draw_upstream(jax.random.fold_in(seeds[6], 71), 0),
    }


EPS = 1e-06

def rounded(values_in):
    return lax.optimization_barrier(values_in.astype(jnp.bfloat16)).astype(jnp.float32)

def to_blocks(array):
    return jnp.swapaxes(array.reshape(SEQS, LEN // TOK_DEV, TOK_DEV, HEADS, DH), 0, 1)

def from_blocks(array):
    return jnp.swapaxes(array, 0, 1).reshape(SEQS, LEN, HEADS * DH)

def reference(queries, keys, values, spikes, gain, upstream):
    width = HEADS * DH
    spiked = keys * spikes.astype(jnp.bfloat16)
    gain_heads = gain.reshape(HEADS, DH)
    causal = jnp.arange(TOK_DEV)[:, None] >= jnp.arange(TOK_DEV)[None, :]
    zero_state = jnp.zeros((SEQS, HEADS, DH, DH), jnp.float32)

    def forward(carry_state, pieces):
        query_block, key_block, value_block, upper_block = [member.astype(jnp.float32) for member in pieces]
        prior_state = rounded(carry_state)
        scores = rounded(jnp.where(causal, jnp.einsum('nthd,nshd->nhts', query_block, key_block), 0.0))
        attended = jnp.einsum('nthd,nhde->nthe', query_block, prior_state) + jnp.einsum('nhts,nshe->nthe', scores, value_block)
        scaled = upper_block * gain_heads
        inv_rms = lax.rsqrt(lax.optimization_barrier(jnp.sum(attended * attended, axis=(2, 3))) / width + EPS)[:, :, None, None]
        cross_mean = lax.optimization_barrier(jnp.sum(scaled * attended, axis=(2, 3)))[:, :, None, None] / width
        grad_attended = rounded(inv_rms * scaled - attended * inv_rms ** 3 * cross_mean)
        gain_part = lax.optimization_barrier(jnp.sum(upper_block * attended * inv_rms, axis=(0, 1)))
        local_grad = jnp.einsum('nthd,nthe->nhde', query_block, grad_attended)
        pair_scores = rounded(jnp.where(causal, jnp.einsum('nthe,nshe->nhts', grad_attended, value_block), 0.0))
        grad_query = jnp.einsum('nthe,nhde->nthd', grad_attended, prior_state) + jnp.einsum('nhts,nshd->nthd', pair_scores, key_block)
        key_inner = jnp.einsum('nhts,nthd->nshd', pair_scores, query_block)
        value_inner = jnp.einsum('nhts,nthe->nshe', scores, grad_attended)
        carry_state = carry_state + jnp.einsum('nshd,nshe->nhde', key_block, value_block)
        return (carry_state, (grad_query.astype(jnp.bfloat16), key_inner, value_inner, local_grad, gain_part))
    final_state, outputs = lax.scan(forward, zero_state, (to_blocks(queries), to_blocks(spiked), to_blocks(values), to_blocks(upstream)))
    grad_query, key_inner, value_inner, local_grads, gain_parts = outputs

    def backward(later_state, pieces):
        key_block, value_block, mask_block, key_part, value_part, local_grad = pieces
        later_rounded = rounded(later_state)
        grad_key = (key_part + jnp.einsum('nshe,nhde->nshd', value_block.astype(jnp.float32), later_rounded)) * mask_block.astype(jnp.float32)
        grad_value = value_part + jnp.einsum('nshd,nhde->nshe', key_block.astype(jnp.float32), later_rounded)
        return (later_state + local_grad, (grad_key.astype(jnp.bfloat16), grad_value.astype(jnp.bfloat16)))
    first_state, grads = lax.scan(backward, zero_state, (to_blocks(spiked), to_blocks(values), to_blocks(spikes), key_inner, value_inner, local_grads), reverse=True)
    grad_key, grad_value = grads
    grad_gain = lax.optimization_barrier(jnp.sum(gain_parts, axis=0)).reshape(width) / math.sqrt(SEQS * LEN)
    return (from_blocks(grad_query), from_blocks(grad_key), from_blocks(grad_value), grad_gain)
```

```python
import functools
import math

import jax
import jax.numpy as jnp
from jax import lax
from jax.experimental import pallas as pl
from jax.experimental.pallas import tpu as pltpu
from jax.sharding import PartitionSpec as P

DH = 128
HEADS = 16
EPS = 1e-06

F32 = jnp.float32
BF16 = jnp.bfloat16
VMEM = pl.BlockSpec(memory_space=pltpu.VMEM)


def dot(a, b, ca, cb):
    return lax.dot_general(a, b, (((ca,), (cb,)), ((), ())), preferred_element_type=F32)


def cols(h):
    return slice(h * DH, (h + 1) * DH)


def call(body, outs, *args, flops=0, moved=0):
    return pl.pallas_call(
        body,
        out_shape=outs,
        in_specs=[VMEM] * len(args),
        out_specs=[VMEM] * len(outs),
        cost_estimate=pl.CostEstimate(flops=flops, bytes_accessed=moved, transcendentals=0),
        compiler_params=pltpu.CompilerParams(vmem_limit_bytes=32 * 2**20),
    )(*args)


def causal_mask(tok):
    rows = lax.broadcasted_iota(jnp.int32, (tok, tok), 0)
    return rows >= lax.broadcasted_iota(jnp.int32, (tok, tok), 1)


def state_kernel(keys, spikes, values, spiked, *states):
    per = states[0].shape[0]
    for h in range(per * len(states)):
        block = keys[0, :, cols(h)] * spikes[0, :, cols(h)].astype(F32).astype(BF16)
        spiked[:, cols(h)] = block
        states[h // per][h % per] = dot(block, values[0, :, cols(h)], 0, 0)


def scores_kernel(queries, spiked, values, scores, intra):
    heads, tok, _ = scores.shape
    causal = causal_mask(tok)
    for h in range(heads):
        raw = dot(queries[0, :, cols(h)], spiked[:, cols(h)], 1, 1)
        block = jnp.where(causal, raw, 0.0).astype(BF16)
        scores[h] = block
        intra[:, cols(h)] = dot(block, values[0, :, cols(h)], 1, 0)


def attend_kernel(queries, intra, upstream, gain, sum_a, sum_b, attended, prior, sums):
    heads = prior.shape[0]
    per = heads // 2
    tok = intra.shape[0]
    square = jnp.zeros((tok, DH), F32)
    cross = jnp.zeros((tok, DH), F32)
    for h in range(heads):
        state = (sum_a if h < per else sum_b)[h % per].astype(BF16)
        prior[h] = state
        block = dot(queries[0, :, cols(h)], state, 1, 0) + intra[:, cols(h)]
        attended[:, cols(h)] = block
        scaled = upstream[0, :, cols(h)].astype(F32) * gain[:, cols(h)]
        square += block * block
        cross += scaled * block
    sums[0:1, :] = jnp.sum(square.T, axis=0, keepdims=True)
    sums[1:2, :] = jnp.sum(cross.T, axis=0, keepdims=True)


def grad_kernel(width, queries, attended, upstream, gain, sums, grad, gain_part, *locals_):
    tok = attended.shape[0]
    per = locals_[0].shape[0]
    inv = lax.rsqrt(sums[0:1, :] / width + EPS)
    factor = inv * inv * inv * (sums[1:2, :] / width)
    inv = jnp.broadcast_to(inv, (DH, tok)).T
    factor = jnp.broadcast_to(factor, (DH, tok)).T
    for h in range(per * len(locals_)):
        block = attended[:, cols(h)]
        upper = upstream[0, :, cols(h)].astype(F32)
        scaled = upper * gain[:, cols(h)]
        result = (inv * scaled - block * factor).astype(BF16)
        grad[:, cols(h)] = result
        gain_part[:, cols(h)] = jnp.sum(upper * block * inv, axis=0, keepdims=True)
        locals_[h // per][h % per] = dot(queries[0, :, cols(h)], result, 0, 0)


def pairs_kernel(queries, spiked, values, grad, prior, scores, grad_query, key_part, value_part):
    heads, tok, _ = scores.shape
    causal = causal_mask(tok)
    for h in range(heads):
        result = grad[:, cols(h)]
        raw = dot(result, values[0, :, cols(h)], 1, 1)
        pairs = jnp.where(causal, raw, 0.0).astype(BF16)
        query_part = dot(result, prior[h], 1, 1) + dot(pairs, spiked[:, cols(h)], 1, 0)
        grad_query[0, :, cols(h)] = query_part.astype(BF16)
        key_part[:, cols(h)] = dot(pairs, queries[0, :, cols(h)], 0, 0)
        value_part[:, cols(h)] = dot(scores[h], result, 0, 0)


def final_kernel(values, spiked, spikes, key_part, value_part, sum_a, sum_b, grad_key, grad_value):
    per = sum_a.shape[0]
    for h in range(2 * per):
        later = (sum_a if h < per else sum_b)[h % per].astype(BF16)
        inner = key_part[:, cols(h)] + dot(values[0, :, cols(h)], later, 1, 1)
        mask = spikes[0, :, cols(h)].astype(F32)
        grad_key[0, :, cols(h)] = (inner * mask).astype(BF16)
        block = value_part[:, cols(h)] + dot(spiked[:, cols(h)], later, 1, 0)
        grad_value[0, :, cols(h)] = block.astype(BF16)


def swap(array, axis, stride):
    size = lax.axis_size(axis)
    return lax.ppermute(array, axis, [(i, i ^ stride) for i in range(size)])


def strides(axis):
    size = lax.axis_size(axis)
    assert size & (size - 1) == 0
    return [1 << k for k in range(size.bit_length() - 1)]


def scan_pair(up, down, axis, reverse):
    at = lax.axis_index(axis)
    order = strides(axis)
    total = up
    up_sum = jnp.zeros_like(up)
    down_sum = jnp.zeros_like(down)
    for small, large in zip(order, order[::-1]):
        from_before = ((at & small) == 0) if reverse else ((at & small) != 0)
        serves_after = ((at & large) != 0) if reverse else ((at & large) == 0)
        if large == order[-1]:
            sent = down
        else:
            sent = down_sum + jnp.where(serves_after, down, 0.0)
        got_down = swap(sent, axis, large)
        got_up = swap(total, axis, small)
        if large == order[-1]:
            got_down = jnp.where(serves_after, 0.0, got_down)
        down_sum = down_sum + got_down
        up_sum = up_sum + jnp.where(from_before, got_up, 0.0)
        total = total + got_up
    return up_sum, down_sum


def per_device(queries, keys, values, spikes, gain, upstream):
    tok = queries.shape[1]
    width_dev = queries.shape[2]
    heads = width_dev // DH
    half = heads // 2
    width = HEADS * DH
    gain_row = gain.reshape(1, width_dev)
    shape = jax.ShapeDtypeStruct
    flat = (tok, width_dev)
    piece = shape((half, DH, DH), F32)
    whole = shape((1, tok, width_dev), BF16)
    small = 2 * heads * tok * DH * DH
    big = 2 * heads * tok * tok * DH

    spiked, state_a, state_b = call(
        state_kernel, [shape(flat, BF16), piece, piece], keys, spikes, values, flops=small, moved=2**20
    )
    scores, intra = call(
        scores_kernel,
        [shape((heads, tok, tok), BF16), shape(flat, F32)],
        queries, spiked, values,
        flops=2 * big, moved=2**21,
    )
    prior_a, prior_b = scan_pair(state_a, state_b, "ctx", False)
    attended, prior, sums = call(
        attend_kernel,
        [shape(flat, F32), shape((heads, DH, DH), BF16), shape((2, tok), F32)],
        queries, intra, upstream, gain_row, prior_a, prior_b,
        flops=small, moved=2**21,
    )
    for stride in strides("head"):
        sums = sums + swap(sums, "head", stride)
    grad, gain_part, local_a, local_b = call(
        functools.partial(grad_kernel, width),
        [shape(flat, BF16), shape((1, width_dev), F32), piece, piece],
        queries, attended, upstream, gain_row, sums,
        flops=small, moved=2**21,
    )
    grad_query, key_part, value_part = call(
        pairs_kernel,
        [whole, shape(flat, F32), shape(flat, F32)],
        queries, spiked, values, grad, prior, scores,
        flops=4 * big + small, moved=2**22,
    )
    later_a, later_b = scan_pair(local_a, local_b, "ctx", True)
    for axis in ("dp", "ctx"):
        for stride in strides(axis):
            gain_part = gain_part + swap(gain_part, axis, stride)
    grad_key, grad_value = call(
        final_kernel,
        [whole, whole],
        values, spiked, spikes, key_part, value_part, later_a, later_b,
        flops=2 * small, moved=2**22,
    )
    total_tokens = tok * lax.axis_size("ctx") * lax.axis_size("dp")
    grad_gain = gain_part.reshape(width_dev) / math.sqrt(total_tokens)
    return grad_query, grad_key, grad_value, grad_gain


def solution(mesh):
    spec = P("dp", "ctx", "head")
    return jax.shard_map(
        per_device,
        mesh=mesh,
        in_specs=(spec, spec, spec, spec, P("head"), spec),
        out_specs=(spec, spec, spec, P("head")),
        check_vma=False,
    )
```

```python
import functools
import math

import jax
import jax.numpy as jnp
from jax import lax
from jax.experimental import pallas as pl
from jax.experimental.pallas import tpu as pltpu
from jax.sharding import PartitionSpec as P

DH = 128
HEADS = 16
EPS = 1e-06

F32 = jnp.float32
BF16 = jnp.bfloat16
VMEM = pl.BlockSpec(memory_space=pltpu.VMEM)
HBM = pl.BlockSpec(memory_space=pltpu.HBM)
GAIN_ROWS = 8


def dot(a, b, ca, cb):
    return lax.dot_general(a, b, (((ca,), (cb,)), ((), ())), preferred_element_type=F32)


def cols(h):
    return slice(h * DH, (h + 1) * DH)


def block_of(pieces, h):
    per = pieces[-1].shape[0] // DH
    return pieces[h // per], cols(h % per)


def call(body, outs, *args, hbm=(), hbm_outs=(), aliases={}, scratch=(), flops=0, moved=0):
    args = [
        pltpu.with_memory_space_constraint(arg, pltpu.HBM) if k in hbm else arg
        for k, arg in enumerate(args)
    ]
    return pl.pallas_call(
        body,
        out_shape=outs,
        in_specs=[HBM if k in hbm else VMEM for k in range(len(args))],
        out_specs=[HBM if k in hbm_outs else VMEM for k in range(len(outs))],
        input_output_aliases=aliases,
        scratch_shapes=scratch,
        cost_estimate=pl.CostEstimate(flops=flops, bytes_accessed=moved, transcendentals=0),
        compiler_params=pltpu.CompilerParams(vmem_limit_bytes=32 * 2**20),
    )(*args)


def causal_mask(tok):
    rows = lax.broadcasted_iota(jnp.int32, (tok, tok), 0)
    return rows >= lax.broadcasted_iota(jnp.int32, (tok, tok), 1)


def score_heads(queries, spiked, values, scores, intra):
    heads, tok, _ = scores.shape
    causal = causal_mask(tok)
    for h in range(heads):
        raw = dot(queries[0, :, cols(h)], spiked[:, cols(h)], 1, 1)
        block = jnp.where(causal, raw, 0.0).astype(BF16)
        scores[h] = block
        intra[:, cols(h)] = dot(block, values[0, :, cols(h)], 1, 0)


def scores_first():
    return lax.axis_index("dp") % 2 == 1


def state_kernel(
    queries, keys, spikes, values, held_queries, spiked, held_values, scores, intra, *rest
):
    *states, key_buf, spike_buf, sems = rest
    heads = spiked.shape[1] // DH
    pairs = (
        (keys, key_buf), (spikes, spike_buf), (values, held_values), (queries, held_queries)
    )
    copies = [pltpu.make_async_copy(src, dst, sems.at[k]) for k, (src, dst) in enumerate(pairs)]
    for copy in copies:
        copy.start()
    for copy in copies[:3]:
        copy.wait()
    for h in range(heads):
        block = key_buf[0, :, cols(h)] * spike_buf[0, :, cols(h)].astype(F32).astype(BF16)
        spiked[:, cols(h)] = block
        ref, rows = block_of(states, h)
        ref[rows, :] = dot(block, held_values[0, :, cols(h)], 0, 0)
    copies[3].wait()

    @pl.when(scores_first())
    def _():
        score_heads(held_queries, spiked, held_values, scores, intra)


def scores_kernel(
    queries, spiked, values, upstream, gain, after, scores_in, intra_in,
    scores, intra, scaled, upper, gain_buf, sems,
):
    del after, scores_in, intra_in
    copies = [
        pltpu.make_async_copy(upstream, upper, sems.at[0]),
        pltpu.make_async_copy(gain, gain_buf, sems.at[1]),
    ]
    for copy in copies:
        copy.start()

    @pl.when(jnp.logical_not(scores_first()))
    def _():
        score_heads(queries, spiked, values, scores, intra)

    for copy in copies:
        copy.wait()
    scaled[...] = upper[0].astype(F32) * gain_buf[...]


def attend_kernel(queries, intra, scaled, sum_a, sum_b, attended, prior, sums):
    heads = prior.shape[0]
    tok = intra.shape[0]
    square = jnp.zeros((tok, DH), F32)
    cross = jnp.zeros((tok, DH), F32)
    for h in range(heads):
        ref, rows = block_of((sum_a, sum_b), h)
        state = ref[rows, :].astype(BF16)
        prior[h] = state
        block = dot(queries[0, :, cols(h)], state, 1, 0) + intra[:, cols(h)]
        attended[:, cols(h)] = block
        square += block * block
        cross += scaled[:, cols(h)] * block
    sums[0:1, :] = jnp.sum(square.T, axis=0, keepdims=True)
    sums[1:2, :] = jnp.sum(cross.T, axis=0, keepdims=True)


def grad_kernel(width, queries, attended, scaled, upper, sums, grad, *locals_):
    tok = attended.shape[0]
    heads = attended.shape[1] // DH
    inv = lax.rsqrt(sums[0:1, :] / width + EPS)
    factor = inv * inv * inv * (sums[1:2, :] / width)
    inv = jnp.broadcast_to(inv, (DH, tok)).T
    factor = jnp.broadcast_to(factor, (DH, tok)).T
    gain_at = locals_[0].shape[0] - GAIN_ROWS
    locals_[0][gain_at:, :] = jnp.zeros((GAIN_ROWS, DH), F32)
    for h in range(heads):
        block = attended[:, cols(h)]
        result = (inv * scaled[:, cols(h)] - block * factor).astype(BF16)
        grad[:, cols(h)] = result
        ref, rows = block_of(locals_, h)
        ref[rows, :] = dot(queries[0, :, cols(h)], result, 0, 0)
        terms = upper[0, :, cols(h)].astype(F32) * block * inv
        locals_[0][gain_at + h : gain_at + h + 1, :] = jnp.sum(terms, axis=0, keepdims=True)


def pairs_kernel(
    queries, spiked, values, grad, prior, scores, after, grad_query, key_part, value_part
):
    del after
    heads, tok, _ = scores.shape
    causal = causal_mask(tok)
    for h in range(heads):
        result = grad[:, cols(h)]
        raw = dot(result, values[0, :, cols(h)], 1, 1)
        pairs = jnp.where(causal, raw, 0.0).astype(BF16)
        query_part = dot(result, prior[h], 1, 1) + dot(pairs, spiked[:, cols(h)], 1, 0)
        grad_query[0, :, cols(h)] = query_part.astype(BF16)
        key_part[:, cols(h)] = dot(pairs, queries[0, :, cols(h)], 0, 0)
        value_part[:, cols(h)] = dot(scores[h], result, 0, 0)


def final_half(first, values, spiked, spikes, key_part, value_part, sums, outs, bufs, sems):
    copies = []
    for h in range(sums.shape[0] // DH):
        at = cols(first + h)
        later = sums[cols(h), :].astype(BF16)
        inner = key_part[:, at] + dot(values[0, :, at], later, 1, 1)
        bufs[0][0, :, cols(h)] = (inner * spikes[0, :, at].astype(F32)).astype(BF16)
        block = value_part[:, at] + dot(spiked[:, at], later, 1, 0)
        bufs[1][0, :, cols(h)] = block.astype(BF16)
        for k in range(2):
            copies.append(
                pltpu.make_async_copy(
                    bufs[k].at[:, :, cols(h)], outs[k].at[:, :, at], sems.at[h, k]
                )
            )
            copies[-1].start()
    return copies


def final_first_kernel(
    values, spiked, spikes, key_part, value_part, sums, grad_key, grad_value, *scratch
):
    *bufs, sems = scratch
    outs = (grad_key, grad_value)
    for copy in final_half(
        0, values, spiked, spikes, key_part, value_part, sums, outs, bufs, sems
    ):
        copy.wait()


def final_last_kernel(
    scale, values, spiked, spikes, key_part, value_part, sums, gain_here, gain_there,
    key_in, value_in, grad_key, grad_value, grad_gain, *scratch,
):
    del key_in, value_in
    *bufs, sems = scratch
    outs = (grad_key, grad_value)
    heads = spiked.shape[1] // DH
    copies = final_half(
        heads // 2, values, spiked, spikes, key_part, value_part, sums, outs, bufs, sems
    )
    for h in range(heads):
        grad_gain[:, cols(h)] = (gain_here[h : h + 1, :] + gain_there[h : h + 1, :]) * scale
    for copy in copies:
        copy.wait()


def swap(array, axis, stride):
    size = lax.axis_size(axis)
    return lax.ppermute(array, axis, [(i, i ^ stride) for i in range(size)])


def strides(axis):
    size = lax.axis_size(axis)
    assert size & (size - 1) == 0
    return [1 << k for k in range(size.bit_length() - 1)]


def scan_pair(up, down, axis, reverse, between, finish=None):
    at = lax.axis_index(axis)
    order = strides(axis)
    total = up
    up_sum = jnp.zeros_like(up)
    down_sum = jnp.zeros_like(down)
    result = None
    for small, large in zip(order, order[::-1]):
        first = large == order[-1]
        from_before = ((at & small) == 0) if reverse else ((at & small) != 0)
        serves_after = ((at & large) != 0) if reverse else ((at & large) == 0)
        sent = down if first else down_sum + jnp.where(serves_after, down, 0.0)
        got_up = swap(total, axis, small)
        got_down = swap(sent, axis, large)
        total = total + got_up
        up_sum = up_sum + jnp.where(from_before, got_up, 0.0)
        if first:
            token, result = between(total)
            got_down, _ = lax.optimization_barrier((got_down, token))
            got_down = jnp.where(serves_after, 0.0, got_down)
        elif small != order[-1] or finish is None:
            got_down, up_sum = lax.optimization_barrier((got_down, up_sum))
        else:
            token, result = finish(up_sum, total, result)
            got_down, _ = lax.optimization_barrier((got_down, token))
        down_sum = down_sum + got_down
    return up_sum, down_sum, result


def per_device(queries, keys, values, spikes, gain, upstream):
    tok = queries.shape[1]
    width_dev = queries.shape[2]
    heads = width_dev // DH
    half = heads // 2
    width = HEADS * DH
    gain_row = gain.reshape(1, width_dev)
    shape = jax.ShapeDtypeStruct
    flat = (tok, width_dev)
    piece = shape((half * DH, DH), F32)
    longer = shape((half * DH + GAIN_ROWS, DH), F32)
    whole = shape((1, tok, width_dev), BF16)
    small = 2 * heads * tok * DH * DH
    big = 2 * heads * tok * tok * DH

    held_queries, spiked, held_values, scores, intra, state_a, state_b = call(
        state_kernel,
        [
            whole, shape(flat, BF16), whole,
            shape((heads, tok, tok), BF16), shape(flat, F32), piece, piece,
        ],
        queries, keys, spikes, values,
        hbm=(0, 1, 2, 3),
        scratch=[
            pltpu.VMEM((1, *flat), BF16),
            pltpu.VMEM((1, *flat), jnp.int32),
            pltpu.SemaphoreType.DMA((4,)),
        ],
        flops=small, moved=2**20,
    )

    def score(total):
        outs = call(
            scores_kernel,
            [shape((heads, tok, tok), BF16), shape(flat, F32), shape(flat, F32), whole],
            held_queries, spiked, held_values, upstream, gain_row, total, scores, intra,
            hbm=(3, 4),
            aliases={6: 0, 7: 1},
            scratch=[pltpu.VMEM((1, width_dev), F32), pltpu.SemaphoreType.DMA((2,))],
            flops=2 * big, moved=2**21,
        )
        return outs[1], outs

    prior_a, prior_b, (scores, intra, scaled, upper) = scan_pair(
        state_a, state_b, "ctx", False, score
    )
    attended, prior, sums = call(
        attend_kernel,
        [shape(flat, F32), shape((heads, DH, DH), BF16), shape((2, tok), F32)],
        held_queries, intra, scaled, prior_a, prior_b,
        flops=small, moved=2**21,
    )
    for stride in strides("head"):
        sums = sums + swap(sums, "head", stride)
    grad, local_a, local_b = call(
        functools.partial(grad_kernel, width),
        [shape(flat, BF16), longer, piece],
        held_queries, attended, scaled, upper, sums,
        flops=small, moved=2**21,
    )

    def pair(total):
        outs = call(
            pairs_kernel,
            [whole, shape(flat, F32), shape(flat, F32)],
            held_queries, spiked, held_values, grad, prior, scores, total,
            flops=4 * big + small, moved=2**22,
        )
        return outs[1], outs

    final_scratch = [pltpu.VMEM((1, tok, half * DH), BF16)] * 2
    final_scratch.append(pltpu.SemaphoreType.DMA((half, 2)))

    def finish(later_a, total, paired):
        grad_query, key_part, value_part = paired
        gain_here = total[half * DH :]
        gain_there = swap(gain_here, "dp", 1)
        first = call(
            final_first_kernel,
            [whole, whole],
            held_values, spiked, spikes, key_part, value_part, later_a,
            hbm_outs=(0, 1),
            scratch=final_scratch,
            flops=small, moved=2**21,
        )
        return first[0], (*paired, gain_here, gain_there, *first)

    _, later_b, (grad_query, key_part, value_part, gain_here, gain_there, *first) = scan_pair(
        local_a, local_b, "ctx", True, pair, finish
    )
    total_tokens = tok * lax.axis_size("ctx") * lax.axis_size("dp")
    grad_key, grad_value, grad_gain = call(
        functools.partial(final_last_kernel, 1.0 / math.sqrt(total_tokens)),
        [whole, whole, shape((1, width_dev), F32)],
        held_values, spiked, spikes, key_part, value_part, later_b, gain_here, gain_there, *first,
        hbm=(8, 9),
        hbm_outs=(0, 1),
        aliases={8: 0, 9: 1},
        scratch=final_scratch,
        flops=small, moved=2**21,
    )
    return grad_query, grad_key, grad_value, grad_gain.reshape(width_dev)


def solution(mesh):
    spec = P("dp", "ctx", "head")
    return jax.shard_map(
        per_device,
        mesh=mesh,
        in_specs=(spec, spec, spec, spec, P("head"), spec),
        out_specs=(spec, spec, spec, P("head")),
        check_vma=False,
    )
```

```python
import functools
import math

import jax
import jax.numpy as jnp
from jax import lax
from jax.experimental import pallas as pl
from jax.experimental.pallas import tpu as pltpu
from jax.sharding import PartitionSpec as P

DH = 128
HEADS = 16
EPS = 1e-06

F32 = jnp.float32
BF16 = jnp.bfloat16
VMEM = pl.BlockSpec(memory_space=pltpu.VMEM)
HBM = pl.BlockSpec(memory_space=pltpu.HBM)
GAIN_ROWS = 8


def dot(a, b, ca, cb):
    return lax.dot_general(a, b, (((ca,), (cb,)), ((), ())), preferred_element_type=F32)


def cols(h):
    return slice(h * DH, (h + 1) * DH)


def block_of(pieces, h):
    per = pieces[-1].shape[0] // DH
    return pieces[h // per], cols(h % per)


def call(body, outs, *args, hbm=(), scratch=(), flops=0, moved=0):
    args = [
        pltpu.with_memory_space_constraint(arg, pltpu.HBM) if k in hbm else arg
        for k, arg in enumerate(args)
    ]
    return pl.pallas_call(
        body,
        out_shape=outs,
        in_specs=[HBM if k in hbm else VMEM for k in range(len(args))],
        out_specs=[VMEM] * len(outs),
        scratch_shapes=scratch,
        cost_estimate=pl.CostEstimate(flops=flops, bytes_accessed=moved, transcendentals=0),
        compiler_params=pltpu.CompilerParams(vmem_limit_bytes=32 * 2**20),
    )(*args)


def causal_mask(tok):
    rows = lax.broadcasted_iota(jnp.int32, (tok, tok), 0)
    return rows >= lax.broadcasted_iota(jnp.int32, (tok, tok), 1)


def state_kernel(
    queries, keys, spikes, values, upstream, held_queries, held_values, upper, spiked, *rest
):
    *states, key_buf, spike_buf, sems = rest
    heads = spiked.shape[1] // DH
    pairs = (
        (keys, key_buf), (spikes, spike_buf), (values, held_values),
        (queries, held_queries), (upstream, upper),
    )
    copies = [pltpu.make_async_copy(src, dst, sems.at[k]) for k, (src, dst) in enumerate(pairs)]
    for copy in copies:
        copy.start()
    for copy in copies[:3]:
        copy.wait()
    for h in range(heads):
        block = key_buf[0, :, cols(h)] * spike_buf[0, :, cols(h)].astype(F32).astype(BF16)
        spiked[:, cols(h)] = block
        ref, rows = block_of(states, h)
        ref[rows, :] = dot(block, held_values[0, :, cols(h)], 0, 0)
    for copy in copies[3:]:
        copy.wait()


def scores_kernel(queries, spiked, values, scores, intra):
    heads, tok, _ = scores.shape
    causal = causal_mask(tok)
    for h in range(heads):
        raw = dot(queries[0, :, cols(h)], spiked[:, cols(h)], 1, 1)
        block = jnp.where(causal, raw, 0.0).astype(BF16)
        scores[h] = block
        intra[:, cols(h)] = dot(block, values[0, :, cols(h)], 1, 0)


def scale_kernel(upper, gain, after, scaled):
    del after
    scaled[...] = upper[0].astype(F32) * gain[...]


def attend_kernel(queries, intra, scaled, sum_a, sum_b, attended, prior, sums):
    heads = prior.shape[0]
    tok = intra.shape[0]
    square = jnp.zeros((tok, DH), F32)
    cross = jnp.zeros((tok, DH), F32)
    for h in range(heads):
        ref, rows = block_of((sum_a, sum_b), h)
        state = ref[rows, :].astype(BF16)
        prior[h] = state
        block = dot(queries[0, :, cols(h)], state, 1, 0) + intra[:, cols(h)]
        attended[:, cols(h)] = block
        square += block * block
        cross += scaled[:, cols(h)] * block
    sums[0:1, :] = jnp.sum(square.T, axis=0, keepdims=True)
    sums[1:2, :] = jnp.sum(cross.T, axis=0, keepdims=True)


def grad_kernel(width, queries, attended, scaled, upper, sums, grad, *locals_):
    tok = attended.shape[0]
    heads = attended.shape[1] // DH
    inv = lax.rsqrt(sums[0:1, :] / width + EPS)
    factor = inv * inv * inv * (sums[1:2, :] / width)
    inv = jnp.broadcast_to(inv, (DH, tok)).T
    factor = jnp.broadcast_to(factor, (DH, tok)).T
    gain_at = locals_[0].shape[0] - GAIN_ROWS
    locals_[0][gain_at:, :] = jnp.zeros((GAIN_ROWS, DH), F32)
    for h in range(heads):
        block = attended[:, cols(h)]
        result = (inv * scaled[:, cols(h)] - block * factor).astype(BF16)
        grad[:, cols(h)] = result
        ref, rows = block_of(locals_, h)
        ref[rows, :] = dot(queries[0, :, cols(h)], result, 0, 0)
        terms = upper[0, :, cols(h)].astype(F32) * block * inv
        locals_[0][gain_at + h : gain_at + h + 1, :] = jnp.sum(terms, axis=0, keepdims=True)


def pair_heads(
    first, to, queries, spiked, values, grad, prior, scores, grad_query, key_part, value_part
):
    tok = spiked.shape[0]
    causal = causal_mask(tok)
    for h in range(key_part.shape[1] // DH):
        at = cols(first + h)
        result = grad[:, at]
        raw = dot(result, values[0, :, at], 1, 1)
        pairs = jnp.where(causal, raw, 0.0).astype(BF16)
        query_part = dot(result, prior[first + h], 1, 1) + dot(pairs, spiked[:, at], 1, 0)
        grad_query[0, :, cols(to + h)] = query_part.astype(BF16)
        key_part[:, cols(h)] = dot(pairs, queries[0, :, at], 0, 0)
        value_part[:, cols(h)] = dot(scores[first + h], result, 0, 0)


def pairs_first_kernel(*refs):
    pair_heads(0, 0, *refs)


def pairs_last_kernel(
    queries, spiked, values, grad, prior, scores, query_half, after,
    grad_query, key_part, value_part,
):
    del after
    done = query_half.shape[2]
    grad_query[:, :, :done] = query_half[...]
    pair_heads(
        done // DH, done // DH, queries, spiked, values, grad, prior, scores,
        grad_query, key_part, value_part,
    )


def final_half(first, values, spiked, spikes, key_part, value_part, sums, outs, to):
    for h in range(sums.shape[0] // DH):
        at = cols(first + h)
        later = sums[cols(h), :].astype(BF16)
        inner = key_part[:, cols(h)] + dot(values[0, :, at], later, 1, 1)
        outs[0][0, :, cols(to + h)] = (inner * spikes[0, :, at].astype(F32)).astype(BF16)
        block = value_part[:, cols(h)] + dot(spiked[:, at], later, 1, 0)
        outs[1][0, :, cols(to + h)] = block.astype(BF16)


def final_first_kernel(
    values, spiked, spikes, key_part, value_part, sums, key_half, value_half
):
    outs = (key_half, value_half)
    final_half(0, values, spiked, spikes, key_part, value_part, sums, outs, 0)


def final_last_kernel(
    scale, values, spiked, spikes, key_part, value_part, sums, gain_here, gain_there,
    key_half, value_half, grad_key, grad_value, grad_gain,
):
    outs = (grad_key, grad_value)
    width = spiked.shape[1]
    done = key_half.shape[2]
    for out, half in zip(outs, (key_half, value_half)):
        out[:, :, :done] = half[...]
    final_half(
        done // DH, values, spiked, spikes, key_part, value_part, sums, outs, done // DH
    )
    for h in range(width // DH):
        grad_gain[:, cols(h)] = (gain_here[h : h + 1, :] + gain_there[h : h + 1, :]) * scale


def swap(array, axis, stride):
    size = lax.axis_size(axis)
    return lax.ppermute(array, axis, [(i, i ^ stride) for i in range(size)])


def gathered_sum(array, axis):
    got = [swap(array, axis, stride) for stride in range(lax.axis_size(axis) - 1, 0, -1)]
    total = array
    for k, other in enumerate(got):
        if k:
            other, total = lax.optimization_barrier((other, total))
        total = total + other
    return total


def strides(axis):
    size = lax.axis_size(axis)
    assert size & (size - 1) == 0
    return [1 << k for k in range(size.bit_length() - 1)]


def swap_by_core(array, axis, even, odd):
    size = lax.axis_size(axis)
    pairs = []
    for core in range(lax.axis_size("dp")):
        stride = odd if core % 2 else even
        pairs += [(core * size + i, core * size + (i ^ stride)) for i in range(size)]
    return lax.ppermute(array, ("dp", axis), pairs)


def scan_pair(lead, last, axis, reverse, by_core, between, finish=None):
    at = lax.axis_index(axis)
    lead_up = lax.axis_index("dp") % 2 == 0 if by_core else jnp.bool_(True)
    up_order = strides(axis)
    down_order = up_order[::-1]
    rounds = len(up_order)
    extra = lax.broadcasted_iota(jnp.int32, lead.shape, 0) >= last.shape[0]
    own = [lead, last]
    goes_up = [lead_up, jnp.logical_not(lead_up)]
    sent = [lead, last]
    total = [lead, last]
    sums = [None, None]
    result = None
    for k in range(rounds):
        up, down = up_order[k], down_order[k]
        got = [
            swap_by_core(sent[0], axis, up, down if by_core else up),
            swap_by_core(sent[1], axis, down, up if by_core else down),
        ]
        for p in range(2):
            stride = jnp.where(goes_up[p], up, down)
            after_partner = ((at & stride) == 0) if reverse else ((at & stride) != 0)
            total[p] = total[p] + got[p]
            if k == 0:
                sums[p] = jnp.where(after_partner, got[p], 0.0)
            else:
                keep = jnp.logical_or(after_partner, jnp.logical_not(goes_up[p]))
                sums[p] = sums[p] + jnp.where(keep, got[p], 0.0)
            if k < rounds - 1:
                next_down = down_order[k + 1]
                serves = ((at & next_down) != 0) if reverse else ((at & next_down) == 0)
                partial = sums[p] + jnp.where(serves, own[p], 0.0)
                whole = jnp.logical_or(goes_up[p], extra) if p == 0 else goes_up[p]
                sent[p] = jnp.where(whole, total[p], partial)
            if p == 0:
                token = sums[0]
                if k == 0:
                    token, result = between(sent[0])
                if k == rounds - 1 and finish is not None:
                    token, result = finish(sums[0], total[0], result)
                got[1], _ = lax.optimization_barrier((got[1], token))
    return sums[0], sums[1], result


def per_device(queries, keys, values, spikes, gain, upstream):
    tok = queries.shape[1]
    width_dev = queries.shape[2]
    heads = width_dev // DH
    half = heads // 2
    width = HEADS * DH
    gain_row = gain.reshape(1, width_dev)
    shape = jax.ShapeDtypeStruct
    flat = (tok, width_dev)
    piece = shape((half * DH, DH), F32)
    longer = shape((half * DH + GAIN_ROWS, DH), F32)
    whole = shape((1, tok, width_dev), BF16)
    small = 2 * heads * tok * DH * DH
    big = 2 * heads * tok * tok * DH

    held_queries, held_values, upper, spiked, state_a, state_b = call(
        state_kernel,
        [whole, whole, whole, shape(flat, BF16), piece, piece],
        queries, keys, spikes, values, upstream,
        hbm=(0, 1, 2, 3, 4),
        scratch=[
            pltpu.VMEM((1, *flat), BF16),
            pltpu.VMEM((1, *flat), jnp.int32),
            pltpu.SemaphoreType.DMA((5,)),
        ],
        flops=small, moved=2**20,
    )
    scores, intra = call(
        scores_kernel,
        [shape((heads, tok, tok), BF16), shape(flat, F32)],
        held_queries, spiked, held_values,
        flops=2 * big, moved=2**21,
    )

    def scale(total):
        scaled = call(scale_kernel, [shape(flat, F32)], upper, gain_row, total, moved=2**20)[0]
        return scaled, scaled

    prior_a, prior_b, scaled = scan_pair(state_a, state_b, "ctx", False, True, scale)
    attended, prior, sums = call(
        attend_kernel,
        [shape(flat, F32), shape((heads, DH, DH), BF16), shape((2, tok), F32)],
        held_queries, intra, scaled, prior_a, prior_b,
        flops=small, moved=2**21,
    )
    sums = gathered_sum(sums, "head")
    grad, local_a, local_b = call(
        functools.partial(grad_kernel, width),
        [shape(flat, BF16), longer, piece],
        held_queries, attended, scaled, upper, sums,
        flops=small, moved=2**21,
    )

    half_outs = [shape((1, tok, half * DH), BF16)] + [shape((tok, half * DH), F32)] * 2
    pair_args = (held_queries, spiked, held_values, grad, prior, scores)
    query_half, *first_parts = call(
        pairs_first_kernel, half_outs, *pair_args, flops=2 * big, moved=2**21
    )

    def pair(total):
        outs = call(
            pairs_last_kernel,
            [whole, *half_outs[1:]],
            *pair_args, query_half, total,
            flops=2 * big, moved=2**21,
        )
        return outs[1], outs

    def finish(later_a, total, paired):
        gain_here = total[half * DH :]
        gain_there = swap(gain_here, "dp", 1)
        first = call(
            final_first_kernel,
            [shape((1, tok, half * DH), BF16)] * 2,
            held_values, spiked, spikes, *first_parts, later_a,
            flops=small, moved=2**21,
        )
        token = (first[0], gain_there)
        return token, (*paired, gain_here, gain_there, *first)

    _, later_b, (grad_query, key_part, value_part, gain_here, gain_there, *first) = scan_pair(
        local_a, local_b, "ctx", True, False, pair, finish
    )
    total_tokens = tok * lax.axis_size("ctx") * lax.axis_size("dp")
    grad_key, grad_value, grad_gain = call(
        functools.partial(final_last_kernel, 1.0 / math.sqrt(total_tokens)),
        [whole, whole, shape((1, width_dev), F32)],
        held_values, spiked, spikes, key_part, value_part, later_b, gain_here, gain_there, *first,
        flops=small, moved=2**21,
    )
    return grad_query, grad_key, grad_value, grad_gain.reshape(width_dev)


def solution(mesh):
    spec = P("dp", "ctx", "head")
    return jax.shard_map(
        per_device,
        mesh=mesh,
        in_specs=(spec, spec, spec, spec, P("head"), spec),
        out_specs=(spec, spec, spec, P("head")),
        check_vma=False,
    )
```

```python
import functools
import math

import jax
import jax.numpy as jnp
from jax import lax
from jax.experimental import pallas as pl
from jax.experimental.pallas import tpu as pltpu
from jax.sharding import PartitionSpec as P

DH = 128
HEADS = 16
EPS = 1e-06

F32 = jnp.float32
BF16 = jnp.bfloat16
VMEM = pl.BlockSpec(memory_space=pltpu.VMEM)
HBM = pl.BlockSpec(memory_space=pltpu.HBM)
GAIN_ROWS = 8


def dot(a, b, ca, cb):
    return lax.dot_general(a, b, (((ca,), (cb,)), ((), ())), preferred_element_type=F32)


def cols(h):
    return slice(h * DH, (h + 1) * DH)


def block_of(pieces, h):
    per = pieces[-1].shape[0] // DH
    return pieces[h // per], cols(h % per)


def call(body, outs, *args, hbm=(), scratch=(), flops=0, moved=0):
    args = [
        pltpu.with_memory_space_constraint(arg, pltpu.HBM) if k in hbm else arg
        for k, arg in enumerate(args)
    ]
    return pl.pallas_call(
        body,
        out_shape=outs,
        in_specs=[HBM if k in hbm else VMEM for k in range(len(args))],
        out_specs=[VMEM] * len(outs),
        scratch_shapes=scratch,
        cost_estimate=pl.CostEstimate(flops=flops, bytes_accessed=moved, transcendentals=0),
        compiler_params=pltpu.CompilerParams(vmem_limit_bytes=32 * 2**20),
    )(*args)


def causal_mask(tok):
    rows = lax.broadcasted_iota(jnp.int32, (tok, tok), 0)
    return rows >= lax.broadcasted_iota(jnp.int32, (tok, tok), 1)


def state_kernel(
    queries, keys, spikes, values, upstream, gain,
    held_queries, held_values, upper, held_gain, spiked, *rest,
):
    *states, key_buf, spike_buf, sems = rest
    heads = spiked.shape[1] // DH
    pairs = (
        (keys, key_buf), (spikes, spike_buf), (values, held_values),
        (queries, held_queries), (upstream, upper), (gain, held_gain),
    )
    copies = [pltpu.make_async_copy(src, dst, sems.at[k]) for k, (src, dst) in enumerate(pairs)]
    for copy in copies:
        copy.start()
    for copy in copies[:3]:
        copy.wait()
    for h in range(heads):
        block = key_buf[0, :, cols(h)] * spike_buf[0, :, cols(h)].astype(F32).astype(BF16)
        spiked[:, cols(h)] = block
        ref, rows = block_of(states, h)
        ref[rows, :] = dot(block, held_values[0, :, cols(h)], 0, 0)
    for copy in copies[3:]:
        copy.wait()


def scores_kernel(queries, spiked, values, scores, intra):
    heads, tok, _ = scores.shape
    causal = causal_mask(tok)
    for h in range(heads):
        raw = dot(queries[0, :, cols(h)], spiked[:, cols(h)], 1, 1)
        block = jnp.where(causal, raw, 0.0).astype(BF16)
        scores[h] = block
        intra[:, cols(h)] = dot(block, values[0, :, cols(h)], 1, 0)


def scale_kernel(upper, gain, after, scaled):
    del after
    scaled[...] = upper[0].astype(F32) * gain[...]


def attend_kernel(queries, intra, scaled, sum_a, sum_b, attended, prior, sums):
    heads = prior.shape[0]
    tok = intra.shape[0]
    square = jnp.zeros((tok, DH), F32)
    cross = jnp.zeros((tok, DH), F32)
    for h in range(heads):
        ref, rows = block_of((sum_a, sum_b), h)
        state = ref[rows, :].astype(BF16)
        prior[h] = state
        block = dot(queries[0, :, cols(h)], state, 1, 0) + intra[:, cols(h)]
        attended[:, cols(h)] = block
        square += block * block
        cross += scaled[:, cols(h)] * block
    sums[0:1, :] = jnp.sum(square.T, axis=0, keepdims=True)
    sums[1:2, :] = jnp.sum(cross.T, axis=0, keepdims=True)


def grad_kernel(width, queries, attended, scaled, upper, sums, grad, *locals_):
    tok = attended.shape[0]
    heads = attended.shape[1] // DH
    inv = lax.rsqrt(sums[0:1, :] / width + EPS)
    factor = inv * inv * inv * (sums[1:2, :] / width)
    inv = jnp.broadcast_to(inv, (DH, tok)).T
    factor = jnp.broadcast_to(factor, (DH, tok)).T
    gain_at = locals_[0].shape[0] - GAIN_ROWS
    locals_[0][gain_at:, :] = jnp.zeros((GAIN_ROWS, DH), F32)
    for h in range(heads):
        block = attended[:, cols(h)]
        result = (inv * scaled[:, cols(h)] - block * factor).astype(BF16)
        grad[:, cols(h)] = result
        ref, rows = block_of(locals_, h)
        ref[rows, :] = dot(queries[0, :, cols(h)], result, 0, 0)
        terms = upper[0, :, cols(h)].astype(F32) * block * inv
        locals_[0][gain_at + h : gain_at + h + 1, :] = jnp.sum(terms, axis=0, keepdims=True)


def pairs_kernel(
    queries, spiked, values, grad, prior, scores,
    grad_query, key_first, value_first, key_last, value_last,
):
    heads, tok, _ = scores.shape
    half = heads // 2
    causal = causal_mask(tok)
    for h in range(heads):
        at = cols(h)
        key_part, value_part = ((key_first, value_first), (key_last, value_last))[h // half]
        result = grad[:, at]
        raw = dot(result, values[0, :, at], 1, 1)
        pairs = jnp.where(causal, raw, 0.0).astype(BF16)
        query_part = dot(result, prior[h], 1, 1) + dot(pairs, spiked[:, at], 1, 0)
        grad_query[0, :, at] = query_part.astype(BF16)
        key_part[:, cols(h % half)] = dot(pairs, queries[0, :, at], 0, 0)
        value_part[:, cols(h % half)] = dot(scores[h], result, 0, 0)


def tail_kernel(total, rows):
    rows[...] = total[total.shape[0] - rows.shape[0] :, :]


def final_half(first, values, spiked, spikes, key_part, value_part, sums, outs, to):
    for h in range(sums.shape[0] // DH):
        at = cols(first + h)
        later = sums[cols(h), :].astype(BF16)
        inner = key_part[:, cols(h)] + dot(values[0, :, at], later, 1, 1)
        outs[0][0, :, cols(to + h)] = (inner * spikes[0, :, at].astype(F32)).astype(BF16)
        block = value_part[:, cols(h)] + dot(spiked[:, at], later, 1, 0)
        outs[1][0, :, cols(to + h)] = block.astype(BF16)


def final_first_kernel(
    values, spiked, spikes, key_part, value_part, sums, key_half, value_half
):
    outs = (key_half, value_half)
    final_half(0, values, spiked, spikes, key_part, value_part, sums, outs, 0)


def final_last_kernel(
    scale, values, spiked, spikes, key_part, value_part, sums, gain_here, gain_there,
    key_half, value_half, grad_key, grad_value, grad_gain,
):
    outs = (grad_key, grad_value)
    width = spiked.shape[1]
    done = key_half.shape[2]
    for out, half in zip(outs, (key_half, value_half)):
        out[:, :, :done] = half[...]
    final_half(
        done // DH, values, spiked, spikes, key_part, value_part, sums, outs, done // DH
    )
    for h in range(width // DH):
        grad_gain[:, cols(h)] = (gain_here[h : h + 1, :] + gain_there[h : h + 1, :]) * scale


def swap(array, axis, stride):
    size = lax.axis_size(axis)
    return lax.ppermute(array, axis, [(i, i ^ stride) for i in range(size)])


def gathered_sum(array, axis):
    got = [swap(array, axis, stride) for stride in range(lax.axis_size(axis) - 1, 0, -1)]
    total = array
    for k, other in enumerate(got):
        if k:
            other, total = lax.optimization_barrier((other, total))
        total = total + other
    return total


def strides(axis):
    size = lax.axis_size(axis)
    assert size & (size - 1) == 0
    return [1 << k for k in range(size.bit_length() - 1)]


def swap_by_core(array, axis, even, odd):
    size = lax.axis_size(axis)
    pairs = []
    for core in range(lax.axis_size("dp")):
        stride = odd if core % 2 else even
        pairs += [(core * size + i, core * size + (i ^ stride)) for i in range(size)]
    return lax.ppermute(array, ("dp", axis), pairs)


def scan_pair(lead, last, axis, reverse, by_core, between, finish=None):
    at = lax.axis_index(axis)
    lead_up = lax.axis_index("dp") % 2 == 0 if by_core else jnp.bool_(True)
    up_order = strides(axis)
    down_order = up_order[::-1]
    rounds = len(up_order)
    own = [lead, last]
    goes_up = [lead_up, jnp.logical_not(lead_up)]
    sent = [lead, last]
    total = [lead, last]
    sums = [None, None]
    result = None
    for k in range(rounds):
        up, down = up_order[k], down_order[k]
        got = [
            swap_by_core(sent[0], axis, up, down if by_core else up),
            swap_by_core(sent[1], axis, down, up if by_core else down),
        ]
        for p in range(2):
            stride = jnp.where(goes_up[p], up, down)
            after_partner = ((at & stride) == 0) if reverse else ((at & stride) != 0)
            total[p] = total[p] + got[p]
            if k == 0:
                sums[p] = jnp.where(after_partner, got[p], 0.0)
            else:
                keep = jnp.logical_or(after_partner, jnp.logical_not(goes_up[p]))
                sums[p] = sums[p] + jnp.where(keep, got[p], 0.0)
            if k < rounds - 1:
                next_down = down_order[k + 1]
                serves = ((at & next_down) != 0) if reverse else ((at & next_down) == 0)
                partial = sums[p] + jnp.where(serves, own[p], 0.0)
                whole = goes_up[p]
                if own[p].shape[0] > last.shape[0]:
                    extra = lax.broadcasted_iota(jnp.int32, own[p].shape, 0) >= last.shape[0]
                    whole = jnp.logical_or(whole, extra)
                sent[p] = jnp.where(whole, total[p], partial)
            if p == 0:
                token = sums[0]
                if k == 0:
                    token, result = between(sent[0])
                elif finish is not None and k < rounds - 1:
                    result = result + got[0][last.shape[0] :]
                elif finish is not None:
                    token, result = finish(sums[0], got[0], result)
                got[1], _ = lax.optimization_barrier((got[1], token))
    return sums[0], sums[1], result


def per_device(queries, keys, values, spikes, gain, upstream):
    tok = queries.shape[1]
    width_dev = queries.shape[2]
    heads = width_dev // DH
    half = heads // 2
    width = HEADS * DH
    gain_row = gain.reshape(1, width_dev)
    shape = jax.ShapeDtypeStruct
    flat = (tok, width_dev)
    piece = shape((half * DH, DH), F32)
    longer = shape((half * DH + GAIN_ROWS, DH), F32)
    whole = shape((1, tok, width_dev), BF16)
    small = 2 * heads * tok * DH * DH
    big = 2 * heads * tok * tok * DH

    held_queries, held_values, upper, held_gain, spiked, state_a, state_b = call(
        state_kernel,
        [whole, whole, whole, shape((1, width_dev), F32), shape(flat, BF16), piece, piece],
        queries, keys, spikes, values, upstream, gain_row,
        hbm=(0, 1, 2, 3, 4, 5),
        scratch=[
            pltpu.VMEM((1, *flat), BF16),
            pltpu.VMEM((1, *flat), jnp.int32),
            pltpu.SemaphoreType.DMA((6,)),
        ],
        flops=small, moved=2**20,
    )
    scores, intra = call(
        scores_kernel,
        [shape((heads, tok, tok), BF16), shape(flat, F32)],
        held_queries, spiked, held_values,
        flops=2 * big, moved=2**21,
    )

    def scale(total):
        scaled = call(scale_kernel, [shape(flat, F32)], upper, held_gain, total, moved=2**20)[0]
        return scaled, scaled

    prior_a, prior_b, scaled = scan_pair(state_a, state_b, "ctx", False, True, scale)
    attended, prior, sums = call(
        attend_kernel,
        [shape(flat, F32), shape((heads, DH, DH), BF16), shape((2, tok), F32)],
        held_queries, intra, scaled, prior_a, prior_b,
        flops=small, moved=2**21,
    )
    sums = gathered_sum(sums, "head")
    grad, local_a, local_b = call(
        functools.partial(grad_kernel, width),
        [shape(flat, BF16), longer, piece],
        held_queries, attended, scaled, upper, sums,
        flops=small, moved=2**21,
    )

    half_part = shape((tok, half * DH), F32)
    grad_query, *parts = call(
        pairs_kernel,
        [whole] + [half_part] * 4,
        held_queries, spiked, held_values, grad, prior, scores,
        flops=4 * big, moved=2**22,
    )

    def gain_rows(total):
        rows = call(tail_kernel, [shape((GAIN_ROWS, DH), F32)], total)[0]
        return rows, rows

    def finish(later_a, got, gain_before):
        gain_here = gain_before + got[half * DH :]
        gain_there = swap(gain_here, "dp", 1)
        first = call(
            final_first_kernel,
            [shape((1, tok, half * DH), BF16)] * 2,
            held_values, spiked, spikes, *parts[:2], later_a,
            flops=small, moved=2**21,
        )
        return (first[0], gain_there), (gain_here, gain_there, *first)

    _, later_b, (gain_here, gain_there, *first) = scan_pair(
        local_a, local_b, "ctx", True, False, gain_rows, finish
    )
    total_tokens = tok * lax.axis_size("ctx") * lax.axis_size("dp")
    grad_key, grad_value, grad_gain = call(
        functools.partial(final_last_kernel, 1.0 / math.sqrt(total_tokens)),
        [whole, whole, shape((1, width_dev), F32)],
        held_values, spiked, spikes, *parts[2:], later_b, gain_here, gain_there, *first,
        flops=small, moved=2**21,
    )
    return grad_query, grad_key, grad_value, grad_gain.reshape(width_dev)


def solution(mesh):
    spec = P("dp", "ctx", "head")
    return jax.shard_map(
        per_device,
        mesh=mesh,
        in_specs=(spec, spec, spec, spec, P("head"), spec),
        out_specs=(spec, spec, spec, P("head")),
        check_vma=False,
    )
```

```python
import functools
import math

import jax
import jax.numpy as jnp
from jax import lax
from jax.experimental import pallas as pl
from jax.experimental.pallas import tpu as pltpu
from jax.sharding import PartitionSpec as P

DH = 128
HEADS = 16
EPS = 1e-06

F32 = jnp.float32
BF16 = jnp.bfloat16
VMEM = pl.BlockSpec(memory_space=pltpu.VMEM)
HBM = pl.BlockSpec(memory_space=pltpu.HBM)
GAIN_ROWS = 8


def dot(a, b, ca, cb):
    return lax.dot_general(a, b, (((ca,), (cb,)), ((), ())), preferred_element_type=F32)


def cols(h):
    return slice(h * DH, (h + 1) * DH)


def block_of(pieces, h):
    per = pieces[-1].shape[0] // DH
    return pieces[h // per], cols(h % per)


def call(body, outs, *args, hbm=(), scratch=(), flops=0, moved=0):
    args = [
        pltpu.with_memory_space_constraint(arg, pltpu.HBM) if k in hbm else arg
        for k, arg in enumerate(args)
    ]
    return pl.pallas_call(
        body,
        out_shape=outs,
        in_specs=[HBM if k in hbm else VMEM for k in range(len(args))],
        out_specs=[VMEM] * len(outs),
        scratch_shapes=scratch,
        cost_estimate=pl.CostEstimate(flops=flops, bytes_accessed=moved, transcendentals=0),
        compiler_params=pltpu.CompilerParams(vmem_limit_bytes=32 * 2**20),
    )(*args)


def causal_mask(tok):
    rows = lax.broadcasted_iota(jnp.int32, (tok, tok), 0)
    return rows >= lax.broadcasted_iota(jnp.int32, (tok, tok), 1)


def state_kernel(
    queries, keys, spikes, values, upstream, gain,
    held_queries, held_values, upper, held_gain, spiked, *rest,
):
    *states, key_buf, spike_buf, sems = rest
    heads = spiked.shape[1] // DH
    pairs = (
        (keys, key_buf), (spikes, spike_buf), (values, held_values),
        (queries, held_queries), (upstream, upper), (gain, held_gain),
    )
    copies = [pltpu.make_async_copy(src, dst, sems.at[k]) for k, (src, dst) in enumerate(pairs)]
    for copy in copies:
        copy.start()
    for copy in copies[:3]:
        copy.wait()
    for h in range(heads):
        block = key_buf[0, :, cols(h)] * spike_buf[0, :, cols(h)].astype(F32).astype(BF16)
        spiked[:, cols(h)] = block
        ref, rows = block_of(states, h)
        ref[rows, :] = dot(block, held_values[0, :, cols(h)], 0, 0)
    for copy in copies[3:]:
        copy.wait()


def scores_kernel(queries, spiked, values, scores, intra):
    heads, tok, _ = scores.shape
    causal = causal_mask(tok)
    for h in range(heads):
        raw = dot(queries[0, :, cols(h)], spiked[:, cols(h)], 1, 1)
        block = jnp.where(causal, raw, 0.0).astype(BF16)
        scores[h] = block
        intra[:, cols(h)] = dot(block, values[0, :, cols(h)], 1, 0)


def scale_kernel(upper, gain, after, scaled):
    del after
    scaled[...] = upper[0].astype(F32) * gain[...]


def attend_kernel(queries, intra, scaled, *rest):
    *states, attended, prior, sums = rest
    heads = prior.shape[0]
    tok = intra.shape[0]
    square = jnp.zeros((tok, DH), F32)
    cross = jnp.zeros((tok, DH), F32)
    for h in range(heads):
        ref, rows = block_of(states, h)
        state = ref[rows, :].astype(BF16)
        prior[h] = state
        block = dot(queries[0, :, cols(h)], state, 1, 0) + intra[:, cols(h)]
        attended[:, cols(h)] = block
        square += block * block
        cross += scaled[:, cols(h)] * block
    sums[0:1, :] = jnp.sum(square.T, axis=0, keepdims=True)
    sums[1:2, :] = jnp.sum(cross.T, axis=0, keepdims=True)


def grad_kernel(width, queries, attended, scaled, upper, sums, grad, *locals_):
    tok = attended.shape[0]
    heads = attended.shape[1] // DH
    inv = lax.rsqrt(sums[0:1, :] / width + EPS)
    factor = inv * inv * inv * (sums[1:2, :] / width)
    inv = jnp.broadcast_to(inv, (DH, tok)).T
    factor = jnp.broadcast_to(factor, (DH, tok)).T
    gain_at = locals_[0].shape[0] - GAIN_ROWS
    locals_[0][gain_at:, :] = jnp.zeros((GAIN_ROWS, DH), F32)
    for h in range(heads):
        block = attended[:, cols(h)]
        result = (inv * scaled[:, cols(h)] - block * factor).astype(BF16)
        grad[:, cols(h)] = result
        ref, rows = block_of(locals_, h)
        ref[rows, :] = dot(queries[0, :, cols(h)], result, 0, 0)
        terms = upper[0, :, cols(h)].astype(F32) * block * inv
        locals_[0][gain_at + h : gain_at + h + 1, :] = jnp.sum(terms, axis=0, keepdims=True)


def pairs_kernel(
    queries, spiked, values, grad, prior, scores,
    grad_query, key_first, value_first, key_last, value_last,
):
    heads, tok, _ = scores.shape
    half = heads // 2
    causal = causal_mask(tok)
    for h in range(heads):
        at = cols(h)
        key_part, value_part = ((key_first, value_first), (key_last, value_last))[h // half]
        result = grad[:, at]
        raw = dot(result, values[0, :, at], 1, 1)
        pairs = jnp.where(causal, raw, 0.0).astype(BF16)
        query_part = dot(result, prior[h], 1, 1) + dot(pairs, spiked[:, at], 1, 0)
        grad_query[0, :, at] = query_part.astype(BF16)
        key_part[:, cols(h % half)] = dot(pairs, queries[0, :, at], 0, 0)
        value_part[:, cols(h % half)] = dot(scores[h], result, 0, 0)


def tail_kernel(total, rows):
    rows[...] = total[total.shape[0] - rows.shape[0] :, :]


def final_heads(first, values, spiked, spikes, key_part, value_part, states, outs, to):
    for h in range(key_part.shape[1] // DH):
        at = cols(first + h)
        ref, rows = block_of(states, h)
        later = ref[rows, :].astype(BF16)
        inner = key_part[:, cols(h)] + dot(values[0, :, at], later, 1, 1)
        outs[0][0, :, cols(to + h)] = (inner * spikes[0, :, at].astype(F32)).astype(BF16)
        block = value_part[:, cols(h)] + dot(spiked[:, at], later, 1, 0)
        outs[1][0, :, cols(to + h)] = block.astype(BF16)


def final_first_kernel(values, spiked, spikes, key_part, value_part, *rest):
    *states, key_half, value_half = rest
    outs = (key_half, value_half)
    final_heads(0, values, spiked, spikes, key_part, value_part, states, outs, 0)


def final_last_kernel(
    scale, values, spiked, spikes, key_part, value_part, gain_here, gain_there,
    key_half, value_half, *rest,
):
    *states, grad_key, grad_value, grad_gain = rest
    outs = (grad_key, grad_value)
    width = spiked.shape[1]
    done = key_half.shape[2]
    for out, half in zip(outs, (key_half, value_half)):
        out[:, :, :done] = half[...]
    first = done // DH
    final_heads(first, values, spiked, spikes, key_part, value_part, states, outs, first)
    for h in range(width // DH):
        grad_gain[:, cols(h)] = (gain_here[h : h + 1, :] + gain_there[h : h + 1, :]) * scale


def swap(array, axis, stride):
    size = lax.axis_size(axis)
    return lax.ppermute(array, axis, [(i, i ^ stride) for i in range(size)])


def gathered_sum(array, axis):
    got = [swap(array, axis, stride) for stride in range(lax.axis_size(axis) - 1, 0, -1)]
    total = array
    for k, other in enumerate(got):
        if k:
            other, total = lax.optimization_barrier((other, total))
        total = total + other
    return total


def strides(axis):
    size = lax.axis_size(axis)
    assert size & (size - 1) == 0
    return [1 << k for k in range(size.bit_length() - 1)]


def swap_by_core(array, axis, even, odd):
    size = lax.axis_size(axis)
    pairs = []
    for core in range(lax.axis_size("dp")):
        stride = odd if core % 2 else even
        pairs += [(core * size + i, core * size + (i ^ stride)) for i in range(size)]
    return lax.ppermute(array, ("dp", axis), pairs)


def scan(pieces, axis, reverse, by_core, between, finish=None):
    at = lax.axis_index(axis)
    up_order = strides(axis)
    down_order = up_order[::-1]
    rounds = len(up_order)
    count = len(pieces)
    rows = pieces[-1].shape[0]
    here_up = lax.axis_index("dp") % 2 == 0 if by_core else jnp.bool_(True)
    first_half = [p < count // 2 for p in range(count)]
    goes_up = [here_up if first else jnp.logical_not(here_up) for first in first_half]
    sent = list(pieces)
    total = list(pieces)
    sums = [None] * count
    result = None
    for k in range(rounds):
        orders = (up_order[k], down_order[k])
        got = []
        for p in range(count):
            even, odd = orders if first_half[p] else orders[::-1]
            got.append(swap_by_core(sent[p], axis, even, odd if by_core else even))
        token = None
        for p in range(count):
            if p:
                got[p], _ = lax.optimization_barrier((got[p], token))
            stride = jnp.where(goes_up[p], *orders)
            after_partner = ((at & stride) == 0) if reverse else ((at & stride) != 0)
            total[p] = total[p] + got[p]
            if k == 0:
                sums[p] = jnp.where(after_partner, got[p], 0.0)
            else:
                keep = jnp.logical_or(after_partner, jnp.logical_not(goes_up[p]))
                sums[p] = sums[p] + jnp.where(keep, got[p], 0.0)
            token = sums[p]
            if k < rounds - 1:
                next_down = down_order[k + 1]
                serves = ((at & next_down) != 0) if reverse else ((at & next_down) == 0)
                partial = sums[p] + jnp.where(serves, pieces[p], 0.0)
                whole = goes_up[p]
                if pieces[p].shape[0] > rows:
                    extra = lax.broadcasted_iota(jnp.int32, pieces[p].shape, 0) >= rows
                    whole = jnp.logical_or(whole, extra)
                token = sent[p] = jnp.where(whole, total[p], partial)
            if p == 0 and k == 0:
                token, result = between(sent[0])
            elif finish is not None and k == rounds - 1:
                token, result = finish(p, sums, got, result)
            elif finish is not None and p == 0:
                result = result + got[0][rows:]
    return sums, result


def per_device(queries, keys, values, spikes, gain, upstream):
    tok = queries.shape[1]
    width_dev = queries.shape[2]
    heads = width_dev // DH
    half = heads // 2
    width = HEADS * DH
    gain_row = gain.reshape(1, width_dev)
    shape = jax.ShapeDtypeStruct
    flat = (tok, width_dev)
    piece = shape((DH, DH), F32)
    half_piece = shape((half * DH, DH), F32)
    longer = shape((half * DH + GAIN_ROWS, DH), F32)
    whole = shape((1, tok, width_dev), BF16)
    small = 2 * heads * tok * DH * DH
    big = 2 * heads * tok * tok * DH

    held_queries, held_values, upper, held_gain, spiked, *states = call(
        state_kernel,
        [whole, whole, whole, shape((1, width_dev), F32), shape(flat, BF16)] + [piece] * heads,
        queries, keys, spikes, values, upstream, gain_row,
        hbm=(0, 1, 2, 3, 4, 5),
        scratch=[
            pltpu.VMEM((1, *flat), BF16),
            pltpu.VMEM((1, *flat), jnp.int32),
            pltpu.SemaphoreType.DMA((6,)),
        ],
        flops=small, moved=2**20,
    )
    def scale(total):
        late, _ = lax.optimization_barrier((spiked, total))
        scaled = call(scale_kernel, [shape(flat, F32)], upper, held_gain, total, moved=2**20)[0]
        scores, intra = call(
            scores_kernel,
            [shape((heads, tok, tok), BF16), shape(flat, F32)],
            held_queries, late, held_values,
            flops=2 * big, moved=2**21,
        )
        return scaled, (scaled, scores, intra)

    priors, (scaled, scores, intra) = scan(states, "ctx", False, True, scale)
    attended, prior, sums = call(
        attend_kernel,
        [shape(flat, F32), shape((heads, DH, DH), BF16), shape((2, tok), F32)],
        held_queries, intra, scaled, *priors,
        flops=small, moved=2**21,
    )
    sums = gathered_sum(sums, "head")
    grad, *locals_ = call(
        functools.partial(grad_kernel, width),
        [shape(flat, BF16), longer, half_piece],
        held_queries, attended, scaled, upper, sums,
        flops=small, moved=2**21,
    )

    half_part = shape((tok, half * DH), F32)
    grad_query, *parts = call(
        pairs_kernel,
        [whole] + [half_part] * 4,
        held_queries, spiked, held_values, grad, prior, scores,
        flops=4 * big, moved=2**22,
    )

    def gain_rows(total):
        rows = call(tail_kernel, [shape((GAIN_ROWS, DH), F32)], total)[0]
        return rows, rows

    def finish(p, sums, got, result):
        if p:
            return sums[p], result
        gain_here = result + got[0][half * DH :]
        gain_there = swap(gain_here, "dp", 1)
        first = call(
            final_first_kernel,
            [shape((1, tok, half * DH), BF16)] * 2,
            held_values, spiked, spikes, *parts[:2], sums[0],
            flops=small, moved=2**21,
        )
        return (first[0], gain_there), (gain_here, gain_there, *first)

    later, ends = scan(locals_, "ctx", True, False, gain_rows, finish)
    total_tokens = tok * lax.axis_size("ctx") * lax.axis_size("dp")
    grad_key, grad_value, grad_gain = call(
        functools.partial(final_last_kernel, 1.0 / math.sqrt(total_tokens)),
        [whole, whole, shape((1, width_dev), F32)],
        held_values, spiked, spikes, *parts[2:], *ends, later[1],
        flops=small, moved=2**21,
    )
    return grad_query, grad_key, grad_value, grad_gain.reshape(width_dev)


def solution(mesh):
    spec = P("dp", "ctx", "head")
    return jax.shard_map(
        per_device,
        mesh=mesh,
        in_specs=(spec, spec, spec, spec, P("head"), spec),
        out_specs=(spec, spec, spec, P("head")),
        check_vma=False,
    )
```

```python
import functools
import math

import jax
import jax.numpy as jnp
from jax import lax
from jax.experimental import pallas as pl
from jax.experimental.pallas import tpu as pltpu
from jax.sharding import PartitionSpec as P

DH = 128
HEADS = 16
EPS = 1e-06

F32 = jnp.float32
BF16 = jnp.bfloat16
VMEM = pl.BlockSpec(memory_space=pltpu.VMEM)
HBM = pl.BlockSpec(memory_space=pltpu.HBM)
GAIN_ROWS = 8


def dot(a, b, ca, cb):
    return lax.dot_general(a, b, (((ca,), (cb,)), ((), ())), preferred_element_type=F32)


def cols(h):
    return slice(h * DH, (h + 1) * DH)


def block_of(pieces, h):
    per = pieces[-1].shape[0] // DH
    return pieces[h // per], cols(h % per)


def call(body, outs, *args, hbm=(), scratch=(), flops=0, moved=0):
    args = [
        pltpu.with_memory_space_constraint(arg, pltpu.HBM) if k in hbm else arg
        for k, arg in enumerate(args)
    ]
    return pl.pallas_call(
        body,
        out_shape=outs,
        in_specs=[HBM if k in hbm else VMEM for k in range(len(args))],
        out_specs=[VMEM] * len(outs),
        scratch_shapes=scratch,
        cost_estimate=pl.CostEstimate(flops=flops, bytes_accessed=moved, transcendentals=0),
        compiler_params=pltpu.CompilerParams(vmem_limit_bytes=32 * 2**20),
    )(*args)


def causal_mask(tok):
    rows = lax.broadcasted_iota(jnp.int32, (tok, tok), 0)
    return rows >= lax.broadcasted_iota(jnp.int32, (tok, tok), 1)


def fetch(pairs, sems, first=0):
    copies = [
        pltpu.make_async_copy(src, dst, sems.at[first + k]) for k, (src, dst) in enumerate(pairs)
    ]
    for copy in copies:
        copy.start()
    return copies


def mask_keys(keys, spikes, spiked):
    for h in range(spiked.shape[1] // DH):
        spiked[:, cols(h)] = keys[0, :, cols(h)] * spikes[0, :, cols(h)].astype(F32).astype(BF16)


def is_last_block():
    return lax.axis_index("ctx") == lax.axis_size("ctx") - 1


def state_kernel(keys, spikes, values, held_values, spiked, *rest):
    *states, key_buf, spike_buf, sems = rest

    @pl.when(is_last_block())
    def _():
        for state in states:
            state[...] = jnp.zeros(state.shape, F32)

    @pl.when(jnp.logical_not(is_last_block()))
    def _():
        pairs = ((keys, key_buf), (spikes, spike_buf), (values, held_values))
        for copy in fetch(pairs, sems):
            copy.wait()
        mask_keys(key_buf, spike_buf, spiked)
        for h in range(spiked.shape[1] // DH):
            ref, rows = block_of(states, h)
            ref[rows, :] = dot(spiked[:, cols(h)], held_values[0, :, cols(h)], 0, 0)


def scores_kernel(
    queries, upstream, gain, keys, spikes, values, values_in, spiked_in,
    held_queries, upper, held_values, spiked, scores, intra, scaled,
    key_buf, spike_buf, gain_buf, sems,
):
    copies = fetch(((queries, held_queries), (upstream, upper), (gain, gain_buf)), sems)

    @pl.when(is_last_block())
    def _():
        pairs = ((keys, key_buf), (spikes, spike_buf), (values, held_values))
        for copy in fetch(pairs, sems, 3):
            copy.wait()
        mask_keys(key_buf, spike_buf, spiked)

    @pl.when(jnp.logical_not(is_last_block()))
    def _():
        held_values[...] = values_in[...]
        spiked[...] = spiked_in[...]

    for copy in copies:
        copy.wait()
    heads, tok, _ = scores.shape
    causal = causal_mask(tok)
    for h in range(heads):
        raw = dot(held_queries[0, :, cols(h)], spiked[:, cols(h)], 1, 1)
        block = jnp.where(causal, raw, 0.0).astype(BF16)
        scores[h] = block
        intra[:, cols(h)] = dot(block, held_values[0, :, cols(h)], 1, 0)
    scaled[...] = upper[0].astype(F32) * gain_buf[...]


def attend_kernel(queries, intra, scaled, *rest):
    *states, attended, prior, sums = rest
    heads = prior.shape[0]
    tok = intra.shape[0]
    square = jnp.zeros((tok, DH), F32)
    cross = jnp.zeros((tok, DH), F32)
    for h in range(heads):
        ref, rows = block_of(states, h)
        state = ref[rows, :].astype(BF16)
        prior[h] = state
        block = dot(queries[0, :, cols(h)], state, 1, 0) + intra[:, cols(h)]
        attended[:, cols(h)] = block
        square += block * block
        cross += scaled[:, cols(h)] * block
    sums[0:1, :] = jnp.sum(square.T, axis=0, keepdims=True)
    sums[1:2, :] = jnp.sum(cross.T, axis=0, keepdims=True)


def grad_kernel(width, queries, attended, scaled, upper, sums, grad, *locals_):
    tok = attended.shape[0]
    heads = attended.shape[1] // DH
    inv = lax.rsqrt(sums[0:1, :] / width + EPS)
    factor = inv * inv * inv * (sums[1:2, :] / width)
    inv = jnp.broadcast_to(inv, (DH, tok)).T
    factor = jnp.broadcast_to(factor, (DH, tok)).T
    gain_at = locals_[0].shape[0] - GAIN_ROWS
    locals_[0][gain_at:, :] = jnp.zeros((GAIN_ROWS, DH), F32)
    for h in range(heads):
        block = attended[:, cols(h)]
        result = (inv * scaled[:, cols(h)] - block * factor).astype(BF16)
        grad[:, cols(h)] = result
        ref, rows = block_of(locals_, h)
        ref[rows, :] = dot(queries[0, :, cols(h)], result, 0, 0)
        terms = upper[0, :, cols(h)].astype(F32) * block * inv
        locals_[0][gain_at + h : gain_at + h + 1, :] = jnp.sum(terms, axis=0, keepdims=True)


def pairs_kernel(
    queries, spiked, values, grad, prior, scores,
    grad_query, key_first, value_first, key_last, value_last,
):
    heads, tok, _ = scores.shape
    half = heads // 2
    causal = causal_mask(tok)
    for h in range(heads):
        at = cols(h)
        key_part, value_part = ((key_first, value_first), (key_last, value_last))[h // half]
        result = grad[:, at]
        raw = dot(result, values[0, :, at], 1, 1)
        pairs = jnp.where(causal, raw, 0.0).astype(BF16)
        query_part = dot(result, prior[h], 1, 1) + dot(pairs, spiked[:, at], 1, 0)
        grad_query[0, :, at] = query_part.astype(BF16)
        key_part[:, cols(h % half)] = dot(pairs, queries[0, :, at], 0, 0)
        value_part[:, cols(h % half)] = dot(scores[h], result, 0, 0)


def tail_kernel(total, rows):
    rows[...] = total[total.shape[0] - rows.shape[0] :, :]


def final_heads(first, values, spiked, spikes, key_part, value_part, states, outs, to):
    for h in range(key_part.shape[1] // DH):
        at = cols(first + h)
        ref, rows = block_of(states, h)
        later = ref[rows, :].astype(BF16)
        inner = key_part[:, cols(h)] + dot(values[0, :, at], later, 1, 1)
        outs[0][0, :, cols(to + h)] = (inner * spikes[0, :, at].astype(F32)).astype(BF16)
        block = value_part[:, cols(h)] + dot(spiked[:, at], later, 1, 0)
        outs[1][0, :, cols(to + h)] = block.astype(BF16)


def final_first_kernel(values, spiked, spikes, key_part, value_part, *rest):
    *states, key_half, value_half = rest
    outs = (key_half, value_half)
    final_heads(0, values, spiked, spikes, key_part, value_part, states, outs, 0)


def final_last_kernel(
    scale, values, spiked, spikes, key_part, value_part, gain_here, gain_there,
    key_half, value_half, *rest,
):
    *states, grad_key, grad_value, grad_gain = rest
    outs = (grad_key, grad_value)
    width = spiked.shape[1]
    done = key_half.shape[2]
    for out, half in zip(outs, (key_half, value_half)):
        out[:, :, :done] = half[...]
    first = done // DH
    final_heads(first, values, spiked, spikes, key_part, value_part, states, outs, first)
    for h in range(width // DH):
        grad_gain[:, cols(h)] = (gain_here[h : h + 1, :] + gain_there[h : h + 1, :]) * scale


def swap(array, axis, stride):
    size = lax.axis_size(axis)
    return lax.ppermute(array, axis, [(i, i ^ stride) for i in range(size)])


def gathered_sum(array, axis):
    got = [swap(array, axis, stride) for stride in range(lax.axis_size(axis) - 1, 0, -1)]
    total = array
    for k, other in enumerate(got):
        if k:
            other, total = lax.optimization_barrier((other, total))
        total = total + other
    return total


def strides(axis):
    size = lax.axis_size(axis)
    assert size & (size - 1) == 0
    return [1 << k for k in range(size.bit_length() - 1)]


def swap_by_core(array, axis, even, odd):
    size = lax.axis_size(axis)
    pairs = []
    for core in range(lax.axis_size("dp")):
        stride = odd if core % 2 else even
        pairs += [(core * size + i, core * size + (i ^ stride)) for i in range(size)]
    return lax.ppermute(array, ("dp", axis), pairs)


def scan(pieces, axis, reverse, by_core, between, finish=None):
    at = lax.axis_index(axis)
    up_order = strides(axis)
    down_order = up_order[::-1]
    rounds = len(up_order)
    count = len(pieces)
    rows = pieces[-1].shape[0]
    here_up = lax.axis_index("dp") % 2 == 0 if by_core else jnp.bool_(True)
    first_half = [p < count // 2 for p in range(count)]
    goes_up = [here_up if first else jnp.logical_not(here_up) for first in first_half]
    sent = list(pieces)
    total = list(pieces)
    sums = [None] * count
    result = None
    for k in range(rounds):
        orders = (up_order[k], down_order[k])
        got = []
        for p in range(count):
            even, odd = orders if first_half[p] else orders[::-1]
            got.append(swap_by_core(sent[p], axis, even, odd if by_core else even))
        token = None
        for p in range(count):
            if p:
                got[p], _ = lax.optimization_barrier((got[p], token))
            stride = jnp.where(goes_up[p], *orders)
            after_partner = ((at & stride) == 0) if reverse else ((at & stride) != 0)
            total[p] = total[p] + got[p]
            if k == 0:
                sums[p] = jnp.where(after_partner, got[p], 0.0)
            else:
                keep = jnp.logical_or(after_partner, jnp.logical_not(goes_up[p]))
                sums[p] = sums[p] + jnp.where(keep, got[p], 0.0)
            token = sums[p]
            if k < rounds - 1:
                next_down = down_order[k + 1]
                serves = ((at & next_down) != 0) if reverse else ((at & next_down) == 0)
                partial = sums[p] + jnp.where(serves, pieces[p], 0.0)
                whole = goes_up[p]
                if pieces[p].shape[0] > rows:
                    extra = lax.broadcasted_iota(jnp.int32, pieces[p].shape, 0) >= rows
                    whole = jnp.logical_or(whole, extra)
                token = sent[p] = jnp.where(whole, total[p], partial)
            if p == 0 and k == 0:
                token, result = between(sent[0])
            elif finish is not None and k == rounds - 1:
                token, result = finish(p, sums, got, result)
            elif finish is not None and p == 0:
                result = result + got[0][rows:]
    return sums, result


def per_device(queries, keys, values, spikes, gain, upstream):
    tok = queries.shape[1]
    width_dev = queries.shape[2]
    heads = width_dev // DH
    half = heads // 2
    width = HEADS * DH
    gain_row = gain.reshape(1, width_dev)
    shape = jax.ShapeDtypeStruct
    flat = (tok, width_dev)
    piece = shape((DH, DH), F32)
    half_piece = shape((half * DH, DH), F32)
    longer = shape((half * DH + GAIN_ROWS, DH), F32)
    whole = shape((1, tok, width_dev), BF16)
    small = 2 * heads * tok * DH * DH
    big = 2 * heads * tok * tok * DH

    early_values, early_spiked, *states = call(
        state_kernel,
        [whole, shape(flat, BF16)] + [piece] * heads,
        keys, spikes, values,
        hbm=(0, 1, 2),
        scratch=[
            pltpu.VMEM((1, *flat), BF16),
            pltpu.VMEM((1, *flat), jnp.int32),
            pltpu.SemaphoreType.DMA((3,)),
        ],
        flops=small, moved=2**20,
    )

    def score(total):
        late, _ = lax.optimization_barrier((early_spiked, total))
        outs = call(
            scores_kernel,
            [
                whole, whole, whole, shape(flat, BF16),
                shape((heads, tok, tok), BF16), shape(flat, F32), shape(flat, F32),
            ],
            queries, upstream, gain_row, keys, spikes, values, early_values, late,
            hbm=(0, 1, 2, 3, 4, 5),
            scratch=[
                pltpu.VMEM((1, *flat), BF16),
                pltpu.VMEM((1, *flat), jnp.int32),
                pltpu.VMEM((1, width_dev), F32),
                pltpu.SemaphoreType.DMA((6,)),
            ],
            flops=2 * big, moved=2**21,
        )
        return total, outs

    priors, (held_queries, upper, held_values, spiked, scores, intra, scaled) = scan(
        states, "ctx", False, True, score
    )
    attended, prior, sums = call(
        attend_kernel,
        [shape(flat, F32), shape((heads, DH, DH), BF16), shape((2, tok), F32)],
        held_queries, intra, scaled, *priors,
        flops=small, moved=2**21,
    )
    sums = gathered_sum(sums, "head")
    grad, *locals_ = call(
        functools.partial(grad_kernel, width),
        [shape(flat, BF16), longer, half_piece],
        held_queries, attended, scaled, upper, sums,
        flops=small, moved=2**21,
    )

    half_part = shape((tok, half * DH), F32)
    grad_query, *parts = call(
        pairs_kernel,
        [whole] + [half_part] * 4,
        held_queries, spiked, held_values, grad, prior, scores,
        flops=4 * big, moved=2**22,
    )

    def gain_rows(total):
        rows = call(tail_kernel, [shape((GAIN_ROWS, DH), F32)], total)[0]
        return rows, rows

    def finish(p, sums, got, result):
        if p:
            return sums[p], result
        gain_here = result + got[0][half * DH :]
        gain_there = swap(gain_here, "dp", 1)
        first = call(
            final_first_kernel,
            [shape((1, tok, half * DH), BF16)] * 2,
            held_values, spiked, spikes, *parts[:2], sums[0],
            flops=small, moved=2**21,
        )
        return (first[0], gain_there), (gain_here, gain_there, *first)

    later, ends = scan(locals_, "ctx", True, False, gain_rows, finish)
    total_tokens = tok * lax.axis_size("ctx") * lax.axis_size("dp")
    grad_key, grad_value, grad_gain = call(
        functools.partial(final_last_kernel, 1.0 / math.sqrt(total_tokens)),
        [whole, whole, shape((1, width_dev), F32)],
        held_values, spiked, spikes, *parts[2:], *ends, later[1],
        flops=small, moved=2**21,
    )
    return grad_query, grad_key, grad_value, grad_gain.reshape(width_dev)


def solution(mesh):
    spec = P("dp", "ctx", "head")
    return jax.shard_map(
        per_device,
        mesh=mesh,
        in_specs=(spec, spec, spec, spec, P("head"), spec),
        out_specs=(spec, spec, spec, P("head")),
        check_vma=False,
    )
```

```python
import functools
import math

import jax
import jax.numpy as jnp
from jax import lax
from jax.experimental import pallas as pl
from jax.experimental.pallas import tpu as pltpu
from jax.sharding import PartitionSpec as P

DH = 128
HEADS = 16
EPS = 1e-06

F32 = jnp.float32
BF16 = jnp.bfloat16
VMEM = pl.BlockSpec(memory_space=pltpu.VMEM)
HBM = pl.BlockSpec(memory_space=pltpu.HBM)
GAIN_ROWS = 8


def dot(a, b, ca, cb):
    return lax.dot_general(a, b, (((ca,), (cb,)), ((), ())), preferred_element_type=F32)


def cols(h):
    return slice(h * DH, (h + 1) * DH)


def block_of(pieces, h):
    per = pieces[-1].shape[0] // DH
    return pieces[h // per], cols(h % per)


def call(body, outs, *args, hbm=(), scratch=(), flops=0, moved=0):
    args = [
        pltpu.with_memory_space_constraint(arg, pltpu.HBM) if k in hbm else arg
        for k, arg in enumerate(args)
    ]
    return pl.pallas_call(
        body,
        out_shape=outs,
        in_specs=[HBM if k in hbm else VMEM for k in range(len(args))],
        out_specs=[VMEM] * len(outs),
        scratch_shapes=scratch,
        cost_estimate=pl.CostEstimate(flops=flops, bytes_accessed=moved, transcendentals=0),
        compiler_params=pltpu.CompilerParams(vmem_limit_bytes=32 * 2**20),
    )(*args)


def causal_mask(tok):
    rows = lax.broadcasted_iota(jnp.int32, (tok, tok), 0)
    return rows >= lax.broadcasted_iota(jnp.int32, (tok, tok), 1)


def fetch(pairs, sems, first=0):
    copies = [
        pltpu.make_async_copy(src, dst, sems.at[first + k]) for k, (src, dst) in enumerate(pairs)
    ]
    for copy in copies:
        copy.start()
    return copies


def mask_keys(keys, spikes, spiked):
    for h in range(spiked.shape[1] // DH):
        spiked[:, cols(h)] = keys[0, :, cols(h)] * spikes[0, :, cols(h)].astype(F32).astype(BF16)


def is_last_block():
    return lax.axis_index("ctx") == lax.axis_size("ctx") - 1


def state_kernel(keys, spikes, values, held_values, spiked, *rest):
    *states, key_buf, spike_buf, sems = rest

    @pl.when(is_last_block())
    def _():
        for state in states:
            state[...] = jnp.zeros(state.shape, F32)

    @pl.when(jnp.logical_not(is_last_block()))
    def _():
        pairs = ((keys, key_buf), (spikes, spike_buf), (values, held_values))
        for copy in fetch(pairs, sems):
            copy.wait()
        mask_keys(key_buf, spike_buf, spiked)
        for h in range(spiked.shape[1] // DH):
            ref, rows = block_of(states, h)
            ref[rows, :] = dot(spiked[:, cols(h)], held_values[0, :, cols(h)], 0, 0)


def scores_kernel(
    queries, upstream, gain, keys, spikes, values, values_in, spiked_in,
    held_queries, upper, held_values, spiked, scores, intra, scaled,
    key_buf, spike_buf, gain_buf, sems,
):
    copies = fetch(((queries, held_queries), (upstream, upper), (gain, gain_buf)), sems)

    @pl.when(is_last_block())
    def _():
        pairs = ((keys, key_buf), (spikes, spike_buf), (values, held_values))
        for copy in fetch(pairs, sems, 3):
            copy.wait()
        mask_keys(key_buf, spike_buf, spiked)

    @pl.when(jnp.logical_not(is_last_block()))
    def _():
        held_values[...] = values_in[...]
        spiked[...] = spiked_in[...]

    for copy in copies:
        copy.wait()
    heads, tok, _ = scores.shape
    causal = causal_mask(tok)
    for h in range(heads):
        raw = dot(held_queries[0, :, cols(h)], spiked[:, cols(h)], 1, 1)
        block = jnp.where(causal, raw, 0.0).astype(BF16)
        scores[h] = block
        intra[:, cols(h)] = dot(block, held_values[0, :, cols(h)], 1, 0)
    scaled[...] = upper[0].astype(F32) * gain_buf[...]


def attend_kernel(queries, intra, scaled, *rest):
    *states, attended, prior, sums = rest
    heads = prior.shape[0]
    tok = intra.shape[0]
    square = jnp.zeros((tok, DH), F32)
    cross = jnp.zeros((tok, DH), F32)
    for h in range(heads):
        ref, rows = block_of(states, h)
        state = ref[rows, :].astype(BF16)
        prior[h] = state
        block = dot(queries[0, :, cols(h)], state, 1, 0) + intra[:, cols(h)]
        attended[:, cols(h)] = block
        square += block * block
        cross += scaled[:, cols(h)] * block
    sums[0:1, :] = jnp.sum(square.T, axis=0, keepdims=True)
    sums[1:2, :] = jnp.sum(cross.T, axis=0, keepdims=True)


def grad_kernel(width, queries, attended, scaled, upper, sums, grad, *locals_):
    tok = attended.shape[0]
    heads = attended.shape[1] // DH
    inv = lax.rsqrt(sums[0:1, :] / width + EPS)
    factor = inv * inv * inv * (sums[1:2, :] / width)
    inv = jnp.broadcast_to(inv, (DH, tok)).T
    factor = jnp.broadcast_to(factor, (DH, tok)).T
    gain_at = locals_[0].shape[0] - GAIN_ROWS
    locals_[0][gain_at:, :] = jnp.zeros((GAIN_ROWS, DH), F32)
    for h in range(heads):
        block = attended[:, cols(h)]
        result = (inv * scaled[:, cols(h)] - block * factor).astype(BF16)
        grad[:, cols(h)] = result
        terms = upper[0, :, cols(h)].astype(F32) * block * inv
        locals_[0][gain_at + h : gain_at + h + 1, :] = jnp.sum(terms, axis=0, keepdims=True)

    @pl.when(lax.axis_index("ctx") == 0)
    def _():
        for h in range(heads):
            ref, rows = block_of(locals_, h)
            ref[rows, :] = jnp.zeros((DH, DH), F32)

    @pl.when(lax.axis_index("ctx") != 0)
    def _():
        for h in range(heads):
            ref, rows = block_of(locals_, h)
            ref[rows, :] = dot(queries[0, :, cols(h)], grad[:, cols(h)], 0, 0)


def pairs_kernel(
    queries, spiked, values, grad, prior, scores,
    grad_query, key_first, value_first, key_last, value_last,
):
    heads, tok, _ = scores.shape
    half = heads // 2
    causal = causal_mask(tok)
    for h in range(heads):
        at = cols(h)
        key_part, value_part = ((key_first, value_first), (key_last, value_last))[h // half]
        result = grad[:, at]
        raw = dot(result, values[0, :, at], 1, 1)
        pairs = jnp.where(causal, raw, 0.0).astype(BF16)
        query_part = dot(result, prior[h], 1, 1) + dot(pairs, spiked[:, at], 1, 0)
        grad_query[0, :, at] = query_part.astype(BF16)
        key_part[:, cols(h % half)] = dot(pairs, queries[0, :, at], 0, 0)
        value_part[:, cols(h % half)] = dot(scores[h], result, 0, 0)


def tail_kernel(total, rows):
    rows[...] = total[total.shape[0] - rows.shape[0] :, :]


def final_heads(first, values, spiked, spikes, key_part, value_part, states, outs, to):
    for h in range(key_part.shape[1] // DH):
        at = cols(first + h)
        ref, rows = block_of(states, h)
        later = ref[rows, :].astype(BF16)
        inner = key_part[:, cols(h)] + dot(values[0, :, at], later, 1, 1)
        outs[0][0, :, cols(to + h)] = (inner * spikes[0, :, at].astype(F32)).astype(BF16)
        block = value_part[:, cols(h)] + dot(spiked[:, at], later, 1, 0)
        outs[1][0, :, cols(to + h)] = block.astype(BF16)


def final_first_kernel(values, spiked, spikes, key_part, value_part, *rest):
    *states, key_half, value_half = rest
    outs = (key_half, value_half)
    final_heads(0, values, spiked, spikes, key_part, value_part, states, outs, 0)


def final_last_kernel(
    scale, values, spiked, spikes, key_part, value_part, gain_here, gain_there,
    key_half, value_half, *rest,
):
    *states, grad_key, grad_value, grad_gain = rest
    outs = (grad_key, grad_value)
    width = spiked.shape[1]
    done = key_half.shape[2]
    for out, half in zip(outs, (key_half, value_half)):
        out[:, :, :done] = half[...]
    first = done // DH
    final_heads(first, values, spiked, spikes, key_part, value_part, states, outs, first)
    for h in range(width // DH):
        grad_gain[:, cols(h)] = (gain_here[h : h + 1, :] + gain_there[h : h + 1, :]) * scale


def swap(array, axis, stride):
    size = lax.axis_size(axis)
    return lax.ppermute(array, axis, [(i, i ^ stride) for i in range(size)])


def gathered_sum(array, axis):
    got = [swap(array, axis, stride) for stride in range(lax.axis_size(axis) - 1, 0, -1)]
    total = array
    for k, other in enumerate(got):
        if k:
            other, total = lax.optimization_barrier((other, total))
        total = total + other
    return total


def strides(axis):
    size = lax.axis_size(axis)
    assert size & (size - 1) == 0
    return [1 << k for k in range(size.bit_length() - 1)]


def swap_by_core(array, axis, even, odd):
    size = lax.axis_size(axis)
    pairs = []
    for core in range(lax.axis_size("dp")):
        stride = odd if core % 2 else even
        pairs += [(core * size + i, core * size + (i ^ stride)) for i in range(size)]
    return lax.ppermute(array, ("dp", axis), pairs)


def scan(pieces, axis, reverse, by_core, between, finish=None):
    at = lax.axis_index(axis)
    up_order = strides(axis)
    down_order = up_order[::-1]
    rounds = len(up_order)
    count = len(pieces)
    rows = pieces[-1].shape[0]
    here_up = lax.axis_index("dp") % 2 == 0 if by_core else jnp.bool_(True)
    first_half = [p < count // 2 for p in range(count)]
    goes_up = [here_up if first else jnp.logical_not(here_up) for first in first_half]
    sent = list(pieces)
    total = list(pieces)
    sums = [None] * count
    result = None
    for k in range(rounds):
        orders = (up_order[k], down_order[k])
        got = []
        for p in range(count):
            even, odd = orders if first_half[p] else orders[::-1]
            got.append(swap_by_core(sent[p], axis, even, odd if by_core else even))
        token = None
        for p in range(count):
            if p:
                got[p], _ = lax.optimization_barrier((got[p], token))
            stride = jnp.where(goes_up[p], *orders)
            after_partner = ((at & stride) == 0) if reverse else ((at & stride) != 0)
            total[p] = total[p] + got[p]
            if k == 0:
                sums[p] = jnp.where(after_partner, got[p], 0.0)
            else:
                keep = jnp.logical_or(after_partner, jnp.logical_not(goes_up[p]))
                sums[p] = sums[p] + jnp.where(keep, got[p], 0.0)
            token = sums[p]
            if k < rounds - 1:
                next_down = down_order[k + 1]
                serves = ((at & next_down) != 0) if reverse else ((at & next_down) == 0)
                partial = sums[p] + jnp.where(serves, pieces[p], 0.0)
                whole = goes_up[p]
                if pieces[p].shape[0] > rows:
                    extra = lax.broadcasted_iota(jnp.int32, pieces[p].shape, 0) >= rows
                    whole = jnp.logical_or(whole, extra)
                token = sent[p] = jnp.where(whole, total[p], partial)
            if p == 0 and k == 0:
                token, result = between(sent[0])
            elif finish is not None and k == rounds - 1:
                token, result = finish(p, sums, got, result)
            elif finish is not None and p == 0:
                result = result + got[0][rows:]
    return sums, result


def per_device(queries, keys, values, spikes, gain, upstream):
    tok = queries.shape[1]
    width_dev = queries.shape[2]
    heads = width_dev // DH
    half = heads // 2
    width = HEADS * DH
    gain_row = gain.reshape(1, width_dev)
    shape = jax.ShapeDtypeStruct
    flat = (tok, width_dev)
    piece = shape((DH, DH), F32)
    half_piece = shape((half * DH, DH), F32)
    longer = shape((half * DH + GAIN_ROWS, DH), F32)
    whole = shape((1, tok, width_dev), BF16)
    small = 2 * heads * tok * DH * DH
    big = 2 * heads * tok * tok * DH

    early_values, early_spiked, *states = call(
        state_kernel,
        [whole, shape(flat, BF16)] + [piece] * heads,
        keys, spikes, values,
        hbm=(0, 1, 2),
        scratch=[
            pltpu.VMEM((1, *flat), BF16),
            pltpu.VMEM((1, *flat), jnp.int32),
            pltpu.SemaphoreType.DMA((3,)),
        ],
        flops=small, moved=2**20,
    )

    def score(total):
        late, _ = lax.optimization_barrier((early_spiked, total))
        outs = call(
            scores_kernel,
            [
                whole, whole, whole, shape(flat, BF16),
                shape((heads, tok, tok), BF16), shape(flat, F32), shape(flat, F32),
            ],
            queries, upstream, gain_row, keys, spikes, values, early_values, late,
            hbm=(0, 1, 2, 3, 4, 5),
            scratch=[
                pltpu.VMEM((1, *flat), BF16),
                pltpu.VMEM((1, *flat), jnp.int32),
                pltpu.VMEM((1, width_dev), F32),
                pltpu.SemaphoreType.DMA((6,)),
            ],
            flops=2 * big, moved=2**21,
        )
        return total, outs

    priors, (held_queries, upper, held_values, spiked, scores, intra, scaled) = scan(
        states, "ctx", False, True, score
    )
    attended, prior, sums = call(
        attend_kernel,
        [shape(flat, F32), shape((heads, DH, DH), BF16), shape((2, tok), F32)],
        held_queries, intra, scaled, *priors,
        flops=small, moved=2**21,
    )
    sums = gathered_sum(sums, "head")
    grad, *locals_ = call(
        functools.partial(grad_kernel, width),
        [shape(flat, BF16), longer, half_piece],
        held_queries, attended, scaled, upper, sums,
        flops=small, moved=2**21,
    )

    half_part = shape((tok, half * DH), F32)
    grad_query, *parts = call(
        pairs_kernel,
        [whole] + [half_part] * 4,
        held_queries, spiked, held_values, grad, prior, scores,
        flops=4 * big, moved=2**22,
    )

    def gain_rows(total):
        rows = call(tail_kernel, [shape((GAIN_ROWS, DH), F32)], total)[0]
        return rows, rows

    def finish(p, sums, got, result):
        if p:
            return sums[p], result
        gain_here = result + got[0][half * DH :]
        gain_there = swap(gain_here, "dp", 1)
        first = call(
            final_first_kernel,
            [shape((1, tok, half * DH), BF16)] * 2,
            held_values, spiked, spikes, *parts[:2], sums[0],
            flops=small, moved=2**21,
        )
        return (first[0], gain_there), (gain_here, gain_there, *first)

    later, ends = scan(locals_, "ctx", True, False, gain_rows, finish)
    total_tokens = tok * lax.axis_size("ctx") * lax.axis_size("dp")
    grad_key, grad_value, grad_gain = call(
        functools.partial(final_last_kernel, 1.0 / math.sqrt(total_tokens)),
        [whole, whole, shape((1, width_dev), F32)],
        held_values, spiked, spikes, *parts[2:], *ends, later[1],
        flops=small, moved=2**21,
    )
    return grad_query, grad_key, grad_value, grad_gain.reshape(width_dev)


def solution(mesh):
    spec = P("dp", "ctx", "head")
    return jax.shard_map(
        per_device,
        mesh=mesh,
        in_specs=(spec, spec, spec, spec, P("head"), spec),
        out_specs=(spec, spec, spec, P("head")),
        check_vma=False,
    )
```

```python
import functools
import math

import jax
import jax.numpy as jnp
from jax import lax
from jax.experimental import pallas as pl
from jax.experimental.pallas import tpu as pltpu
from jax.sharding import PartitionSpec as P

DH = 128
HEADS = 16
EPS = 1e-06

F32 = jnp.float32
BF16 = jnp.bfloat16
VMEM = pl.BlockSpec(memory_space=pltpu.VMEM)
HBM = pl.BlockSpec(memory_space=pltpu.HBM)
GAIN_ROWS = 8


def dot(a, b, ca, cb):
    return lax.dot_general(a, b, (((ca,), (cb,)), ((), ())), preferred_element_type=F32)


def cols(h):
    return slice(h * DH, (h + 1) * DH)


def block_of(pieces, h):
    per = pieces[-1].shape[0] // DH
    return pieces[h // per], cols(h % per)


def call(body, outs, *args, hbm=(), scratch=(), flops=0, moved=0):
    args = [
        pltpu.with_memory_space_constraint(arg, pltpu.HBM) if k in hbm else arg
        for k, arg in enumerate(args)
    ]
    return pl.pallas_call(
        body,
        out_shape=outs,
        in_specs=[HBM if k in hbm else VMEM for k in range(len(args))],
        out_specs=[VMEM] * len(outs),
        scratch_shapes=scratch,
        cost_estimate=pl.CostEstimate(flops=flops, bytes_accessed=moved, transcendentals=0),
        compiler_params=pltpu.CompilerParams(vmem_limit_bytes=32 * 2**20),
    )(*args)


def causal_mask(tok):
    rows = lax.broadcasted_iota(jnp.int32, (tok, tok), 0)
    return rows >= lax.broadcasted_iota(jnp.int32, (tok, tok), 1)


def fetch(pairs, sems, first=0):
    copies = [
        pltpu.make_async_copy(src, dst, sems.at[first + k]) for k, (src, dst) in enumerate(pairs)
    ]
    for copy in copies:
        copy.start()
    return copies


def mask_keys(keys, spikes, spiked):
    for h in range(spiked.shape[1] // DH):
        spiked[:, cols(h)] = keys[0, :, cols(h)] * spikes[0, :, cols(h)].astype(F32).astype(BF16)


def is_last_block():
    return lax.axis_index("ctx") == lax.axis_size("ctx") - 1


def state_kernel(keys, spikes, values, held_values, spiked, *rest):
    *states, key_buf, spike_buf, sems = rest

    @pl.when(is_last_block())
    def _():
        for state in states:
            state[...] = jnp.zeros(state.shape, F32)

    @pl.when(jnp.logical_not(is_last_block()))
    def _():
        pairs = ((keys, key_buf), (spikes, spike_buf), (values, held_values))
        for copy in fetch(pairs, sems):
            copy.wait()
        mask_keys(key_buf, spike_buf, spiked)
        for h in range(spiked.shape[1] // DH):
            ref, rows = block_of(states, h)
            ref[rows, :] = dot(spiked[:, cols(h)], held_values[0, :, cols(h)], 0, 0)


def scores_kernel(
    queries, upstream, gain, keys, spikes, values, values_in, spiked_in,
    held_queries, upper, held_values, spiked, scores, intra, scaled,
    key_buf, spike_buf, gain_buf, sems,
):
    copies = fetch(((queries, held_queries), (upstream, upper), (gain, gain_buf)), sems)

    @pl.when(is_last_block())
    def _():
        pairs = ((keys, key_buf), (spikes, spike_buf), (values, held_values))
        for copy in fetch(pairs, sems, 3):
            copy.wait()
        mask_keys(key_buf, spike_buf, spiked)

    @pl.when(jnp.logical_not(is_last_block()))
    def _():
        held_values[...] = values_in[...]
        spiked[...] = spiked_in[...]

    for copy in copies:
        copy.wait()
    heads, tok, _ = scores.shape
    causal = causal_mask(tok)
    for h in range(heads):
        raw = dot(held_queries[0, :, cols(h)], spiked[:, cols(h)], 1, 1)
        block = jnp.where(causal, raw, 0.0).astype(BF16)
        scores[h] = block
        intra[:, cols(h)] = dot(block, held_values[0, :, cols(h)], 1, 0)
    scaled[...] = upper[0].astype(F32) * gain_buf[...]


def attend_kernel(queries, intra, scaled, *rest):
    *states, attended, prior, sums = rest
    heads = prior.shape[0]
    tok = intra.shape[0]

    def attend(first_block):
        square = jnp.zeros((tok, DH), F32)
        cross = jnp.zeros((tok, DH), F32)
        for h in range(heads):
            block = intra[:, cols(h)]
            if first_block:
                prior[h] = jnp.zeros((DH, DH), BF16)
            else:
                ref, rows = block_of(states, h)
                state = ref[rows, :].astype(BF16)
                prior[h] = state
                block = dot(queries[0, :, cols(h)], state, 1, 0) + block
            attended[:, cols(h)] = block
            square += block * block
            cross += scaled[:, cols(h)] * block
        sums[0:1, :] = jnp.sum(square.T, axis=0, keepdims=True)
        sums[1:2, :] = jnp.sum(cross.T, axis=0, keepdims=True)

    at = lax.axis_index("ctx")
    pl.when(at == 0)(functools.partial(attend, True))
    pl.when(at != 0)(functools.partial(attend, False))


def grad_kernel(width, queries, attended, scaled, upper, sums, grad, *locals_):
    tok = attended.shape[0]
    heads = attended.shape[1] // DH
    inv = lax.rsqrt(sums[0:1, :] / width + EPS)
    factor = inv * inv * inv * (sums[1:2, :] / width)
    inv = jnp.broadcast_to(inv, (DH, tok)).T
    factor = jnp.broadcast_to(factor, (DH, tok)).T
    gain_at = locals_[0].shape[0] - GAIN_ROWS
    locals_[0][gain_at:, :] = jnp.zeros((GAIN_ROWS, DH), F32)
    for h in range(heads):
        block = attended[:, cols(h)]
        result = (inv * scaled[:, cols(h)] - block * factor).astype(BF16)
        grad[:, cols(h)] = result
        terms = upper[0, :, cols(h)].astype(F32) * block * inv
        locals_[0][gain_at + h : gain_at + h + 1, :] = jnp.sum(terms, axis=0, keepdims=True)

    @pl.when(lax.axis_index("ctx") == 0)
    def _():
        for h in range(heads):
            ref, rows = block_of(locals_, h)
            ref[rows, :] = jnp.zeros((DH, DH), F32)

    @pl.when(lax.axis_index("ctx") != 0)
    def _():
        for h in range(heads):
            ref, rows = block_of(locals_, h)
            ref[rows, :] = dot(queries[0, :, cols(h)], grad[:, cols(h)], 0, 0)


def pairs_kernel(
    queries, spiked, values, grad, prior, scores,
    grad_query, key_first, value_first, key_last, value_last,
):
    heads, tok, _ = scores.shape
    half = heads // 2
    causal = causal_mask(tok)
    for h in range(heads):
        at = cols(h)
        key_part, value_part = ((key_first, value_first), (key_last, value_last))[h // half]
        result = grad[:, at]
        raw = dot(result, values[0, :, at], 1, 1)
        pairs = jnp.where(causal, raw, 0.0).astype(BF16)
        query_part = dot(result, prior[h], 1, 1) + dot(pairs, spiked[:, at], 1, 0)
        grad_query[0, :, at] = query_part.astype(BF16)
        key_part[:, cols(h % half)] = dot(pairs, queries[0, :, at], 0, 0)
        value_part[:, cols(h % half)] = dot(scores[h], result, 0, 0)


def tail_kernel(total, rows):
    rows[...] = total[total.shape[0] - rows.shape[0] :, :]


def final_heads(first, values, spiked, spikes, key_part, value_part, states, outs, to):
    for h in range(key_part.shape[1] // DH):
        at = cols(first + h)
        ref, rows = block_of(states, h)
        later = ref[rows, :].astype(BF16)
        inner = key_part[:, cols(h)] + dot(values[0, :, at], later, 1, 1)
        outs[0][0, :, cols(to + h)] = (inner * spikes[0, :, at].astype(F32)).astype(BF16)
        block = value_part[:, cols(h)] + dot(spiked[:, at], later, 1, 0)
        outs[1][0, :, cols(to + h)] = block.astype(BF16)


def final_first_kernel(values, spiked, spikes, key_part, value_part, *rest):
    *states, key_half, value_half = rest
    outs = (key_half, value_half)
    final_heads(0, values, spiked, spikes, key_part, value_part, states, outs, 0)


def final_last_kernel(
    scale, values, spiked, spikes, key_part, value_part, gain_here, gain_there,
    key_half, value_half, *rest,
):
    *states, grad_key, grad_value, grad_gain = rest
    outs = (grad_key, grad_value)
    width = spiked.shape[1]
    done = key_half.shape[2]
    for out, half in zip(outs, (key_half, value_half)):
        out[:, :, :done] = half[...]
    first = done // DH
    final_heads(first, values, spiked, spikes, key_part, value_part, states, outs, first)
    for h in range(width // DH):
        grad_gain[:, cols(h)] = (gain_here[h : h + 1, :] + gain_there[h : h + 1, :]) * scale


def swap(array, axis, stride):
    size = lax.axis_size(axis)
    return lax.ppermute(array, axis, [(i, i ^ stride) for i in range(size)])


def gathered_sum(array, axis):
    got = [swap(array, axis, stride) for stride in range(lax.axis_size(axis) - 1, 0, -1)]
    total = array
    for k, other in enumerate(got):
        if k:
            other, total = lax.optimization_barrier((other, total))
        total = total + other
    return total


def strides(axis):
    size = lax.axis_size(axis)
    assert size & (size - 1) == 0
    return [1 << k for k in range(size.bit_length() - 1)]


def swap_by_core(array, axis, even, odd):
    size = lax.axis_size(axis)
    pairs = []
    for core in range(lax.axis_size("dp")):
        stride = odd if core % 2 else even
        pairs += [(core * size + i, core * size + (i ^ stride)) for i in range(size)]
    return lax.ppermute(array, ("dp", axis), pairs)


def scan(pieces, axis, reverse, by_core, between, finish=None):
    at = lax.axis_index(axis)
    up_order = strides(axis)
    down_order = up_order[::-1]
    rounds = len(up_order)
    count = len(pieces)
    rows = pieces[-1].shape[0]
    here_up = lax.axis_index("dp") % 2 == 0 if by_core else jnp.bool_(True)
    first_half = [p < count // 2 for p in range(count)]
    goes_up = [here_up if first else jnp.logical_not(here_up) for first in first_half]
    sent = list(pieces)
    total = list(pieces)
    sums = [None] * count
    result = None
    for k in range(rounds):
        orders = (up_order[k], down_order[k])
        got = []
        for p in range(count):
            even, odd = orders if first_half[p] else orders[::-1]
            got.append(swap_by_core(sent[p], axis, even, odd if by_core else even))
        token = None
        for p in range(count):
            if p:
                got[p], _ = lax.optimization_barrier((got[p], token))
            stride = jnp.where(goes_up[p], *orders)
            after_partner = ((at & stride) == 0) if reverse else ((at & stride) != 0)
            total[p] = total[p] + got[p]
            if k == 0:
                sums[p] = jnp.where(after_partner, got[p], 0.0)
            else:
                keep = jnp.logical_or(after_partner, jnp.logical_not(goes_up[p]))
                sums[p] = sums[p] + jnp.where(keep, got[p], 0.0)
            token = sums[p]
            if k < rounds - 1:
                next_down = down_order[k + 1]
                serves = ((at & next_down) != 0) if reverse else ((at & next_down) == 0)
                partial = sums[p] + jnp.where(serves, pieces[p], 0.0)
                whole = goes_up[p]
                if pieces[p].shape[0] > rows:
                    extra = lax.broadcasted_iota(jnp.int32, pieces[p].shape, 0) >= rows
                    whole = jnp.logical_or(whole, extra)
                token = sent[p] = jnp.where(whole, total[p], partial)
            if p == 0 and k == 0:
                token, result = between(sent[0])
            elif finish is not None and k == rounds - 1:
                token, result = finish(p, sums, got, result)
            elif finish is not None and p == 0:
                result = result + got[0][rows:]
    return sums, result


def per_device(queries, keys, values, spikes, gain, upstream):
    tok = queries.shape[1]
    width_dev = queries.shape[2]
    heads = width_dev // DH
    half = heads // 2
    width = HEADS * DH
    gain_row = gain.reshape(1, width_dev)
    shape = jax.ShapeDtypeStruct
    flat = (tok, width_dev)
    piece = shape((DH, DH), F32)
    half_piece = shape((half * DH, DH), F32)
    longer = shape((half * DH + GAIN_ROWS, DH), F32)
    whole = shape((1, tok, width_dev), BF16)
    small = 2 * heads * tok * DH * DH
    big = 2 * heads * tok * tok * DH

    early_values, early_spiked, *states = call(
        state_kernel,
        [whole, shape(flat, BF16)] + [piece] * heads,
        keys, spikes, values,
        hbm=(0, 1, 2),
        scratch=[
            pltpu.VMEM((1, *flat), BF16),
            pltpu.VMEM((1, *flat), jnp.int32),
            pltpu.SemaphoreType.DMA((3,)),
        ],
        flops=small, moved=2**20,
    )

    def score(total):
        late, _ = lax.optimization_barrier((early_spiked, total))
        outs = call(
            scores_kernel,
            [
                whole, whole, whole, shape(flat, BF16),
                shape((heads, tok, tok), BF16), shape(flat, F32), shape(flat, F32),
            ],
            queries, upstream, gain_row, keys, spikes, values, early_values, late,
            hbm=(0, 1, 2, 3, 4, 5),
            scratch=[
                pltpu.VMEM((1, *flat), BF16),
                pltpu.VMEM((1, *flat), jnp.int32),
                pltpu.VMEM((1, width_dev), F32),
                pltpu.SemaphoreType.DMA((6,)),
            ],
            flops=2 * big, moved=2**21,
        )
        return total, outs

    priors, (held_queries, upper, held_values, spiked, scores, intra, scaled) = scan(
        states, "ctx", False, True, score
    )
    attended, prior, sums = call(
        attend_kernel,
        [shape(flat, F32), shape((heads, DH, DH), BF16), shape((2, tok), F32)],
        held_queries, intra, scaled, *priors,
        flops=small, moved=2**21,
    )
    sums = gathered_sum(sums, "head")
    grad, *locals_ = call(
        functools.partial(grad_kernel, width),
        [shape(flat, BF16), longer, half_piece],
        held_queries, attended, scaled, upper, sums,
        flops=small, moved=2**21,
    )

    half_part = shape((tok, half * DH), F32)
    grad_query, *parts = call(
        pairs_kernel,
        [whole] + [half_part] * 4,
        held_queries, spiked, held_values, grad, prior, scores,
        flops=4 * big, moved=2**22,
    )

    def gain_rows(total):
        rows = call(tail_kernel, [shape((GAIN_ROWS, DH), F32)], total)[0]
        return rows, rows

    def finish(p, sums, got, result):
        if p:
            return sums[p], result
        gain_here = result + got[0][half * DH :]
        gain_there = swap(gain_here, "dp", 1)
        first = call(
            final_first_kernel,
            [shape((1, tok, half * DH), BF16)] * 2,
            held_values, spiked, spikes, *parts[:2], sums[0],
            flops=small, moved=2**21,
        )
        return (first[0], gain_there), (gain_here, gain_there, *first)

    later, ends = scan(locals_, "ctx", True, False, gain_rows, finish)
    total_tokens = tok * lax.axis_size("ctx") * lax.axis_size("dp")
    grad_key, grad_value, grad_gain = call(
        functools.partial(final_last_kernel, 1.0 / math.sqrt(total_tokens)),
        [whole, whole, shape((1, width_dev), F32)],
        held_values, spiked, spikes, *parts[2:], *ends, later[1],
        flops=small, moved=2**21,
    )
    return grad_query, grad_key, grad_value, grad_gain.reshape(width_dev)


def solution(mesh):
    spec = P("dp", "ctx", "head")
    return jax.shard_map(
        per_device,
        mesh=mesh,
        in_specs=(spec, spec, spec, spec, P("head"), spec),
        out_specs=(spec, spec, spec, P("head")),
        check_vma=False,
    )
```
